512 devices in a mesh: dom: 4 (over z_lo), seq: 32 (over x, y, core), rep: 4 (over z_hi).
Axes of the slice: x: 4, y: 4, z: 16 (z_hi: 4, z_lo: 4; z = z_hi * 4 + z_lo), core: 2. Of those that a mesh axis runs over, the one named last changes fastest.
Arguments:
- counts: int32 [32], P('rep'), parts along dimension 0, may hold values from 0 to 4, as said below
- video_query: bfloat16 [32, 1536, 2048], P(('rep', 'dom'), 'seq'), parts along dimension 0, may hold values from -21 to 21
- video_key: bfloat16 [32, 1536, 2048], P(('rep', 'dom'), 'seq'), parts along dimension 0, may hold values from -10.2 to 10.2
- video_value: bfloat16 [32, 1536, 2048], P(('rep', 'dom'), 'seq'), parts along dimension 0, may hold values from -6 to 6
- text_query: bfloat16 [32, 256, 2048], P(('rep', 'dom'), 'seq'), parts along dimension 0, may hold values from -6 to 6
- text_key: bfloat16 [32, 256, 2048], P(('rep', 'dom'), 'seq'), parts along dimension 0, may hold values from -6 to 6
- text_value: bfloat16 [32, 256, 2048], P(('rep', 'dom'), 'seq'), parts along dimension 0, may hold values from -6 to 6
- fresh_noise: bfloat16 [32, 1536, 2048], P(('rep', 'dom'), 'seq'), parts along dimension 0, may hold values from -6 to 6
Outputs:
- video_out: bfloat16 [32, 1536, 2048], P(('rep', 'dom'), 'seq'), parts along dimension 0
- text_out: bfloat16 [32, 256, 2048], P(('rep', 'dom'), 'seq'), parts along dimension 0
The draws below stay inside these ranges and needn't reach their ends.
There are 4 independent parts, one for each index of `rep`. The reference program is written for one: setup_inputs(seed, part) draws one part's arguments, and reference() takes and returns one part's arrays. A program takes and returns all parts, laid end to end along the dimension named above; each array names one. Nothing has to cross between parts.
Inputs may be any that keep to these rules, and one draw needn't show every extreme that they name: counts sum to 8; some particle has exactly 4 offspring; particles 0 to 1 together have more than 4 offspring.
All inputs are finite; a program needn't handle non-finite values.
Results may differ from the reference program's by a relative error of at most 0.005.
Values may be sent and summed in bfloat16 or wider, within the bound.
No kernel may reach another device: no remote copies, remote signals or barrier semaphores. Data moves between devices by JAX's collectives and lax.ppermute only.
A program may use at most 64 MiB of HBM per device.

```python
import jax
import jax.numpy as jnp
from jax import lax

PARTICLES = 8
HEADS = 16
HD = 128
VTOK = 1536
TXT = 256
SEQ_ALL = 1792


def draw_counts(key, part):
    key = jax.random.fold_in(key, 1)
    quarter = PARTICLES // 4
    heavy = jax.random.randint(jax.random.fold_in(key, 2), (), 0, quarter).astype(jnp.int32)
    offset = jax.random.randint(jax.random.fold_in(key, 6), (), 0, quarter - 1).astype(jnp.int32)
    forced = (heavy + 1 + offset) % quarter
    others = jax.random.randint(jax.random.fold_in(key, 3), (PARTICLES // 2 - 1,), 0, PARTICLES - 1)
    others = others + (others >= heavy).astype(jnp.int32)
    slot_ids = jnp.arange(PARTICLES, dtype=jnp.int32)
    spread = jnp.sum((others[:, None] == slot_ids[None, :]).astype(jnp.int32), axis=0)
    spread = spread + (slot_ids == forced).astype(jnp.int32)
    return (spread + PARTICLES // 2 * (slot_ids == heavy).astype(jnp.int32)).astype(jnp.int32)


def draw_video_key(key, part):
    key = jax.random.fold_in(key, 4)
    full_shape = (PARTICLES, VTOK, HEADS * HD)
    values = jnp.clip(1.7 * jax.random.normal(key, full_shape, jnp.float32), -10.2, 10.2)
    return values.astype(jnp.bfloat16)


def draw_video_query(key, part):
    key = jax.random.fold_in(key, 5)
    full_shape = (PARTICLES, VTOK, HEADS * HD)
    values = jnp.clip(1.7 * jax.random.normal(key, full_shape, jnp.float32), -10.2, 10.2)
    return values.astype(jnp.bfloat16)


def levels(stream_key, extent, pieces, smallest, high):
    level = 1.0
    for position, shards_of in pieces:
        heights = jax.random.uniform(jax.random.fold_in(jax.random.fold_in(stream_key, 6), position), (shards_of,), jnp.float32, smallest / len(pieces), high / len(pieces))
        level = level * jnp.repeat(jnp.exp(heights), extent[position] // shards_of).reshape((-1,) + (1,) * (len(extent) - 1 - position))
    return level


def normal_values(key, dims, scale, reach, pieces=(), kind=jnp.bfloat16):
    level = levels(key, dims, pieces, -0.22, 0.18) if pieces else 1.0
    entries = jax.random.normal(key, dims, jnp.float32) * scale * level
    return jnp.minimum(jnp.maximum(entries, -reach), reach).astype(kind)


def setup_inputs(seed: int = 0, part: int = 0) -> dict:
    keys = jax.random.split(jax.random.key(seed), 9)
    part_splits = jax.random.split(jax.random.fold_in(keys[8], part), 9)
    counts = draw_counts(jax.random.fold_in(jax.random.fold_in(keys[8], part), 71), part)
    video_query = draw_video_query(jax.random.fold_in(jax.random.fold_in(keys[8], part), 71), part)
    video_key = draw_video_key(jax.random.fold_in(jax.random.fold_in(keys[8], part), 71), part)
    video_value = normal_values(part_splits[3], (PARTICLES, VTOK, HEADS * HD), 1.0, 6.0, ((0, 4), (1, 32)))
    text_query = normal_values(part_splits[4], (PARTICLES, TXT, HEADS * HD), 1.7, 6.0, ((0, 4), (1, 32)))
    text_key = normal_values(part_splits[5], (PARTICLES, TXT, HEADS * HD), 1.7, 6.0, ((0, 4), (1, 32)))
    text_value = normal_values(part_splits[6], (PARTICLES, TXT, HEADS * HD), 1.0, 6.0, ((0, 4), (1, 32)))
    fresh_noise = normal_values(part_splits[7], (PARTICLES, VTOK, HEADS * HD), 0.5, 6.0, ((0, 4), (1, 32)))
    return {"counts": counts, "video_query": video_query, "video_key": video_key, "video_value": video_value, "text_query": text_query, "text_key": text_key, "text_value": text_value, "fresh_noise": fresh_noise}


def ancestors(counts):
    running = jnp.cumsum(counts).astype(jnp.int32)
    slot_ids = jnp.arange(counts.shape[0], dtype=jnp.int32)
    return jnp.sum((running[None, :] <= slot_ids[:, None]).astype(jnp.int32), axis=1).astype(jnp.int32)


def attend(queries, key_rows, value_rows):
    scores = lax.dot_general(queries, key_rows, (((1,), (1,)), ((), ())), preferred_element_type=jnp.float32)
    scores = scores * (queries.shape[1] ** -0.5)
    row_max = jnp.max(scores, axis=1, keepdims=True)
    weights = jnp.exp(scores - row_max)
    row_sum = jnp.sum(weights, axis=1, keepdims=True)
    rounded = (weights / row_sum).astype(jnp.bfloat16)
    return jnp.dot(rounded, value_rows, preferred_element_type=jnp.float32).astype(jnp.bfloat16)


def reference(counts, video_query, video_key, video_value, text_query, text_key, text_value, fresh_noise):
    lineage = ancestors(counts)

    def head_major(video_part, text_part):
        joined = jnp.concatenate([video_part, text_part], axis=1)
        joined = joined.reshape(PARTICLES, SEQ_ALL, HEADS, HD).transpose(0, 2, 1, 3)
        return joined.reshape(PARTICLES * HEADS, SEQ_ALL, HD)

    queries = head_major(video_query, text_query)
    key_rows = head_major(video_key, text_key)
    value_rows = head_major(video_value, text_value)

    def single(member):
        return attend(member[0], member[1], member[2])

    attended = lax.map(single, (queries, key_rows, value_rows))
    attended = attended.reshape(PARTICLES, HEADS, SEQ_ALL, HD).transpose(0, 2, 1, 3)
    attended = attended.reshape(PARTICLES, SEQ_ALL, HEADS * HD)
    chosen = jnp.take(attended, lineage, axis=0)
    video_part = lax.optimization_barrier(chosen[:, :VTOK])
    video_out = (video_part.astype(jnp.float32) + fresh_noise.astype(jnp.float32)).astype(jnp.bfloat16)
    return video_out, chosen[:, VTOK:]
```

```python
import functools

import jax
import jax.numpy as jnp
from jax import lax
from jax.experimental import pallas as pl
from jax.experimental.pallas import tpu as pltpu
from jax.sharding import PartitionSpec as P

HD = 128
LOG2E = 1.4426950408889634
VMEM_LIMIT = 48 * 2**20


def ancestors(counts):
    running = jnp.cumsum(counts)
    slot_ids = jnp.arange(counts.shape[0], dtype=jnp.int32)
    return jnp.sum((running[None, :] <= slot_ids[:, None]).astype(jnp.int32), axis=1)


def pack_kernel(vq, vk, vv, tq, tk, tv, out):
    rows, text = vq.shape[1], tq.shape[1]
    base = 3 * rows
    for p in range(vq.shape[0]):
        for h in range(vq.shape[2] // HD):
            columns = slice(h * HD, (h + 1) * HD)
            for i, ref in enumerate((vq, vk, vv)):
                out[p, h, i * rows : (i + 1) * rows, :] = ref[p, :, columns]
            for i, ref in enumerate((tq, tk, tv)):
                out[p, h, base + i * text : base + (i + 1) * text, :] = ref[p, :, columns]


def pack(vq, vk, vv, tq, tk, tv, steps=2):
    resident, rows, features = vq.shape
    text = tq.shape[1]
    heads = features // HD
    width = features // steps
    total = 3 * (rows + text)
    video = pl.BlockSpec((resident, rows, width), lambda i: (0, 0, i))
    words = pl.BlockSpec((resident, text, width), lambda i: (0, 0, i))
    packed = pl.pallas_call(
        pack_kernel,
        grid=(steps,),
        in_specs=[video] * 3 + [words] * 3,
        out_specs=pl.BlockSpec((resident, heads // steps, total, HD), lambda i: (0, i, 0, 0)),
        out_shape=jax.ShapeDtypeStruct((resident, heads, total, HD), vq.dtype),
        name="pack",
    )(vq, vk, vv, tq, tk, tv)
    return packed.reshape(resident * heads, total, HD)


def attend_kernel(x, out, q, k, v, *, rows, text, block):
    n = x.shape[0]
    video_rows, text_rows = n * rows, n * text
    total = video_rows + text_rows
    base = 3 * rows
    for i, ref in enumerate((q, k, v)):
        ref[0:video_rows, 0:HD] = x[:, i * rows : (i + 1) * rows, :].reshape(video_rows, HD)
        ref[video_rows:total, 0:HD] = x[:, base + i * text : base + (i + 1) * text, :].reshape(
            text_rows, HD
        )
    v[:, HD : 2 * HD] = jnp.ones((total, HD), v.dtype)
    scale = HD**-0.5 * LOG2E
    for start in range(0, total, block):
        piece = q[start : start + block, :]
        scores = lax.dot_general(
            piece, k[...], (((1,), (1,)), ((), ())), preferred_element_type=jnp.float32
        )
        row_max = jnp.max(scores, axis=1, keepdims=True)
        weights = jnp.exp2((scores - row_max) * scale).astype(v.dtype)
        summed = jnp.dot(weights, v[...], preferred_element_type=jnp.float32)
        q[start : start + block, :] = (summed[:, :HD] / summed[:, HD:]).astype(q.dtype)
    out[:, 0:rows, :] = q[0:video_rows, :].reshape(n, rows, HD)
    out[:, rows : rows + text, :] = q[video_rows:total, :].reshape(n, text, HD)


def attend(x, rows, text, block=256):
    n = x.shape[0]
    total = n * (rows + text)
    return pl.pallas_call(
        functools.partial(attend_kernel, rows=rows, text=text, block=block),
        in_specs=[pl.BlockSpec(memory_space=pltpu.VMEM)],
        out_specs=pl.BlockSpec(memory_space=pltpu.VMEM),
        out_shape=jax.ShapeDtypeStruct((n, rows + text, HD), x.dtype),
        scratch_shapes=[
            pltpu.VMEM((total, HD), x.dtype),
            pltpu.VMEM((total, HD), x.dtype),
            pltpu.VMEM((total, 2 * HD), x.dtype),
        ],
        compiler_params=pltpu.CompilerParams(vmem_limit_bytes=VMEM_LIMIT),
        name="attend",
    )(x)


def fetch(choice, slot, candidates, target, sem):
    start = 0
    for ref in candidates:
        for b in range(ref.shape[0]):

            @pl.when(choice[slot] == start + b)
            def _(ref=ref, b=b):
                pltpu.make_async_copy(ref.at[b], target, sem).start()

        start += ref.shape[0]


def select_kernel(choice, *refs):
    candidates, out, sems = refs[:-2], refs[-2], refs[-1]
    for s in range(out.shape[0]):
        fetch(choice, s, candidates, out.at[s], sems.at[s])
    for s in range(out.shape[0]):
        pltpu.make_async_copy(out.at[s], out.at[s], sems.at[s]).wait()


def select(choice, candidates):
    slots = choice.shape[0]
    return pl.pallas_call(
        select_kernel,
        grid_spec=pltpu.PrefetchScalarGridSpec(
            num_scalar_prefetch=1,
            grid=(1,),
            in_specs=[pl.BlockSpec(memory_space=pl.ANY)] * len(candidates),
            out_specs=pl.BlockSpec(memory_space=pl.ANY),
            scratch_shapes=[pltpu.SemaphoreType.DMA((slots,))],
        ),
        out_shape=jax.ShapeDtypeStruct((slots,) + candidates[0].shape[1:], candidates[0].dtype),
        name="select",
    )(choice, *candidates)


def finish_kernel(choice, *refs):
    candidates, (noise, video, words, held, sems) = refs[:-5], refs[-5:]
    slots, rows = noise.shape[0], noise.shape[1]
    text = words.shape[1]
    for s in range(slots):
        fetch(choice, s, candidates, held.at[s], sems.at[s])
    for s in range(slots):
        pltpu.make_async_copy(held.at[s], held.at[s], sems.at[s]).wait()
        for h in range(held.shape[1]):
            columns = slice(h * HD, (h + 1) * HD)
            total = held[s, h, 0:rows, :].astype(jnp.float32) + noise[s, :, columns].astype(
                jnp.float32
            )
            video[s, :, columns] = total.astype(video.dtype)
            words[s, :, columns] = held[s, h, rows : rows + text, :]


def finish(choice, candidates, noise, text):
    slots, rows, features = noise.shape
    whole = lambda *shape: pl.BlockSpec(shape, lambda i, c: (0, 0, 0))
    return pl.pallas_call(
        finish_kernel,
        grid_spec=pltpu.PrefetchScalarGridSpec(
            num_scalar_prefetch=1,
            grid=(1,),
            in_specs=[pl.BlockSpec(memory_space=pl.ANY)] * len(candidates)
            + [whole(slots, rows, features)],
            out_specs=[whole(slots, rows, features), whole(slots, text, features)],
            scratch_shapes=[
                pltpu.VMEM((slots,) + candidates[0].shape[1:], candidates[0].dtype),
                pltpu.SemaphoreType.DMA((slots,)),
            ],
        ),
        out_shape=[
            jax.ShapeDtypeStruct(noise.shape, noise.dtype),
            jax.ShapeDtypeStruct((slots, text, features), noise.dtype),
        ],
        name="finish",
    )(choice, *candidates, noise)


def per_device(
    counts, video_query, video_key, video_value, text_query, text_key, text_value, fresh_noise
):
    resident, rows, features = video_query.shape
    text = text_query.shape[1]
    heads = features // HD
    lineage = ancestors(counts)
    dom = lax.axis_index("dom")

    packed = pack(video_query, video_key, video_value, text_query, text_key, text_value)
    gathered = lax.all_to_all(packed, "seq", split_axis=0, concat_axis=0, tiled=True)
    attended = attend(gathered, rows, text)
    returned = lax.all_to_all(attended, "seq", split_axis=0, concat_axis=0, tiled=True)
    own = returned.reshape(resident, heads, rows + text, HD)

    near = lax.ppermute(own, "dom", [(0, 1), (1, 2)])
    second = lax.ppermute(own[1:], "dom", [(0, 2)])
    mine = lax.dynamic_slice_in_dim(lineage, dom * resident, resident)
    tail = lineage[6:8]
    onward = jnp.where(tail == 1, 4, jnp.where(tail < 4, tail, jnp.where(tail < 6, tail - 4, 0)))
    onward = jnp.where(dom == 2, onward, jnp.arange(resident, dtype=jnp.int32))
    last = lax.ppermute(select(onward, (own, near, second)), "dom", [(2, 3), (3, 2)])
    place = jnp.arange(resident, dtype=jnp.int32)
    choice = jnp.where(
        dom == 0,
        mine,
        jnp.where(
            dom == 1,
            mine + 2,
            jnp.where(
                dom == 2,
                jnp.where(
                    mine == 1, 4, jnp.where(mine < 4, mine, jnp.where(mine < 6, mine - 4, mine - 1))
                ),
                jnp.where(mine < 6, 5 + place, mine - 6),
            ),
        ),
    )
    video_out, text_out = finish(choice, (own, near, second, last), fresh_noise, text)
    return video_out, text_out


def solution(mesh):
    placed = P(("rep", "dom"), "seq", None)
    return jax.shard_map(
        per_device,
        mesh=mesh,
        in_specs=(P("rep"),) + (placed,) * 7,
        out_specs=(placed, placed),
        check_vma=False,
    )
```

```python
import functools
import itertools

import jax
import jax.numpy as jnp
from jax import lax
from jax.experimental import pallas as pl
from jax.experimental.pallas import tpu as pltpu
from jax.sharding import PartitionSpec as P

HD = 128
LOG2E = 1.4426950408889634
VMEM_LIMIT = 48 * 2**20


def lineages(slots):
    half = slots // 2
    rows = set()
    for other in range(1, half + 1):
        for first, second in ((half, other), (other, half)):
            rest = slots - first - second
            for tail in itertools.combinations_with_replacement(range(2, slots), rest):
                rows.add((0,) * first + (1,) * second + tail)
    return sorted(rows)


def transfers(row):
    pairs = []
    for plane in range(1, len(row) // 2):
        wanted = sorted(set(row[2 * plane : 2 * plane + 2]))
        pairs += [(p // 2, plane) for p in wanted if p // 2 != plane]
    return tuple(sorted(pairs))


def key_of(row):
    as_int = lambda flag: jnp.where(flag, 1, 0) if isinstance(flag, jax.Array) else int(flag)
    key = as_int(row[2] != row[3])
    key = key + 2 * as_int(row[5] // 2 == 1) + 4 * as_int(row[5] // 2 == 3)
    key = key + 8 * as_int(row[6] // 2 == 0)
    for plane, weight in ((1, 16), (2, 48)):
        from_six = as_int(row[6] // 2 == plane)
        from_seven = as_int(row[7] // 2 == plane)
        same = as_int(row[6] == row[7])
        key = key + weight * (from_six + from_seven - from_six * same)
    return key


def plans(slots):
    found = {}
    for row in lineages(slots):
        found[key_of(row)] = transfers(row)
    out = []
    for key in sorted(found):
        rounds = []
        seen = {}
        for pair in sorted(found[key], key=lambda p: -abs(p[1] - p[0])):
            which = seen.get(pair, 0)
            seen[pair] = which + 1
            for members in rounds:
                if all(pair[0] != m[0] and pair[1] != m[1] for m in members):
                    members.append(pair + (which,))
                    break
            else:
                rounds.append([pair + (which,)])
        out.append((key, rounds))
    return out


def pack_kernel(counts, vq, vk, vv, tq, tk, tv, out, facts, *, keys):
    @pl.when(pl.program_id(0) == 0)
    def _():
        slots = counts.shape[0]
        running = [counts[0]]
        for i in range(1, slots):
            running.append(running[-1] + counts[i])
        row = [sum(jnp.where(r <= j, 1, 0) for r in running) for j in range(slots)]
        facts[0] = lax.axis_index("dom")
        for j in range(slots):
            facts[1 + j] = row[j]
        key = key_of(row)
        facts[1 + slots] = sum(jnp.where(key == k, i, 0) for i, k in enumerate(keys))

    rows, text = vq.shape[1], tq.shape[1]
    base = 3 * rows
    for p in range(vq.shape[0]):
        for h in range(vq.shape[2] // HD):
            columns = slice(h * HD, (h + 1) * HD)
            for i, ref in enumerate((vq, vk, vv)):
                out[p, h, i * rows : (i + 1) * rows, :] = ref[p, :, columns]
            for i, ref in enumerate((tq, tk, tv)):
                out[p, h, base + i * text : base + (i + 1) * text, :] = ref[p, :, columns]


def pack(counts, vq, vk, vv, tq, tk, tv, keys, steps=2):
    resident, rows, features = vq.shape
    text = tq.shape[1]
    heads = features // HD
    width = features // steps
    total = 3 * (rows + text)
    video = pl.BlockSpec((resident, rows, width), lambda i: (0, 0, i))
    words = pl.BlockSpec((resident, text, width), lambda i: (0, 0, i))
    scalars = pl.BlockSpec(memory_space=pltpu.SMEM)
    packed, facts = pl.pallas_call(
        functools.partial(pack_kernel, keys=keys),
        grid=(steps,),
        in_specs=[scalars] + [video] * 3 + [words] * 3,
        out_specs=[
            pl.BlockSpec((resident, heads // steps, total, HD), lambda i: (0, i, 0, 0)),
            scalars,
        ],
        out_shape=[
            jax.ShapeDtypeStruct((resident, heads, total, HD), vq.dtype),
            jax.ShapeDtypeStruct((counts.shape[0] + 2,), jnp.int32),
        ],
        name="pack",
    )(counts, vq, vk, vv, tq, tk, tv)
    return packed.reshape(resident * heads, total, HD), facts


def attend_kernel(x, out, q, k, v, *, rows, text, block):
    n = x.shape[0]
    video_rows, text_rows = n * rows, n * text
    total = video_rows + text_rows
    base = 3 * rows
    for i, ref in enumerate((q, k, v)):
        ref[0:video_rows, 0:HD] = x[:, i * rows : (i + 1) * rows, :].reshape(video_rows, HD)
        ref[video_rows:total, 0:HD] = x[:, base + i * text : base + (i + 1) * text, :].reshape(
            text_rows, HD
        )
    v[:, HD : 2 * HD] = jnp.ones((total, HD), v.dtype)
    scale = HD**-0.5 * LOG2E
    for start in range(0, total, block):
        piece = q[start : start + block, :]
        scores = lax.dot_general(
            piece, k[...], (((1,), (1,)), ((), ())), preferred_element_type=jnp.float32
        )
        row_max = jnp.max(scores, axis=1, keepdims=True)
        weights = jnp.exp2((scores - row_max) * scale).astype(v.dtype)
        summed = jnp.dot(weights, v[...], preferred_element_type=jnp.float32)
        q[start : start + block, :] = (summed[:, :HD] / summed[:, HD:]).astype(q.dtype)
    out[:, 0:rows, :] = q[0:video_rows, :].reshape(n, rows, HD)
    out[:, rows : rows + text, :] = q[video_rows:total, :].reshape(n, text, HD)


def attend(x, rows, text, block=256):
    n = x.shape[0]
    total = n * (rows + text)
    return pl.pallas_call(
        functools.partial(attend_kernel, rows=rows, text=text, block=block),
        in_specs=[pl.BlockSpec(memory_space=pltpu.VMEM)],
        out_specs=pl.BlockSpec(memory_space=pltpu.VMEM),
        out_shape=jax.ShapeDtypeStruct((n, rows + text, HD), x.dtype),
        scratch_shapes=[
            pltpu.VMEM((total, HD), x.dtype),
            pltpu.VMEM((total, HD), x.dtype),
            pltpu.VMEM((total, 2 * HD), x.dtype),
        ],
        compiler_params=pltpu.CompilerParams(vmem_limit_bytes=VMEM_LIMIT),
        name="attend",
    )(x)


def outgoing_kernel(facts, own, *sends, rounds):
    dom = facts[0]
    for members, send in zip(rounds, sends):
        index = 0
        for source, target, which in members:
            slot = 1 + 2 * target
            if which == 0:
                wanted = jnp.where(facts[slot] // 2 == source, facts[slot], facts[slot + 1])
            else:
                wanted = facts[slot + 1]
            index = jnp.where(dom == source, lax.rem(wanted, 2), index)
        send[...] = own[index]


def outgoing(facts, own, rounds):
    vmem = pl.BlockSpec(memory_space=pltpu.VMEM)
    block = jax.ShapeDtypeStruct(own.shape[1:], own.dtype)
    return pl.pallas_call(
        functools.partial(outgoing_kernel, rounds=rounds),
        in_specs=[pl.BlockSpec(memory_space=pltpu.SMEM), vmem],
        out_specs=[vmem] * len(rounds),
        out_shape=[block] * len(rounds),
        name="outgoing",
    )(facts, own)


def finish_kernel(facts, own, *refs, rounds):
    received, (noise, video, words) = refs[:-3], refs[-3:]
    slots, rows = noise.shape[0], noise.shape[1]
    text = words.shape[1]
    dom = facts[0]
    for s in range(slots):
        ancestor = facts[1 + 2 * dom + s]
        origin = ancestor // 2
        chosen = 0
        for r, members in enumerate(rounds):
            for source, target, which in members:
                twice = sum(m[:2] == (source, target) for ms in rounds for m in ms) == 2
                if not twice or which == s:
                    hit = jnp.logical_and(dom == target, origin == source)
                    chosen = jnp.where(hit, 1 + r, chosen)

        def write(block, s=s):
            for h in range(own.shape[1]):
                columns = slice(h * HD, (h + 1) * HD)
                part = block[h, 0:rows, :].astype(jnp.float32)
                total = part + noise[s, :, columns].astype(jnp.float32)
                video[s, :, columns] = total.astype(video.dtype)
                words[s, :, columns] = block[h, rows : rows + text, :]

        @pl.when(chosen == 0)
        def _(write=write, ancestor=ancestor):
            write(own.at[lax.rem(ancestor, 2)])

        for r, block in enumerate(received):

            @pl.when(chosen == 1 + r)
            def _(write=write, block=block):
                write(block)


def finish(facts, own, received, noise, text, rounds):
    slots, _, features = noise.shape
    vmem = pl.BlockSpec(memory_space=pltpu.VMEM)
    return pl.pallas_call(
        functools.partial(finish_kernel, rounds=rounds),
        in_specs=[pl.BlockSpec(memory_space=pltpu.SMEM)] + [vmem] * (2 + len(received)),
        out_specs=[vmem, vmem],
        out_shape=[
            jax.ShapeDtypeStruct(noise.shape, noise.dtype),
            jax.ShapeDtypeStruct((slots, text, features), noise.dtype),
        ],
        name="finish",
    )(facts, own, *received, noise)


def resample(rounds, text, facts, own, noise):
    sends = outgoing(facts, own, rounds)
    received = [
        lax.ppermute(send, "dom", [m[:2] for m in members]) for send, members in zip(sends, rounds)
    ]
    return tuple(finish(facts, own, received, noise, text, rounds))


def per_device(
    counts, video_query, video_key, video_value, text_query, text_key, text_value, fresh_noise
):
    resident, rows, features = video_query.shape
    text = text_query.shape[1]
    heads = features // HD
    known = plans(counts.shape[0])

    packed, facts = pack(
        counts,
        video_query,
        video_key,
        video_value,
        text_query,
        text_key,
        text_value,
        [key for key, _ in known],
    )
    gathered = lax.all_to_all(packed, "seq", split_axis=0, concat_axis=0, tiled=True)
    attended = attend(gathered, rows, text)
    returned = lax.all_to_all(attended, "seq", split_axis=0, concat_axis=0, tiled=True)
    own = returned.reshape(resident, heads, rows + text, HD)
    branches = [functools.partial(resample, rounds, text) for _, rounds in known]
    return lax.switch(facts[counts.shape[0] + 1], branches, facts, own, fresh_noise)


def solution(mesh):
    placed = P(("rep", "dom"), "seq", None)
    return jax.shard_map(
        per_device,
        mesh=mesh,
        in_specs=(P("rep"),) + (placed,) * 7,
        out_specs=(placed, placed),
        check_vma=False,
    )
```

```python
import functools
import itertools

import jax
import jax.numpy as jnp
from jax import lax
from jax.experimental import pallas as pl
from jax.experimental.pallas import tpu as pltpu
from jax.sharding import PartitionSpec as P

HD = 128
LOG2E = 1.4426950408889634
VMEM_LIMIT = 32 * 2**20
SMALL = 16 * 2**20


def lineages(slots):
    half = slots // 2
    rows = set()
    for other in range(1, half + 1):
        for first, second in ((half, other), (other, half)):
            rest = slots - first - second
            for tail in itertools.combinations_with_replacement(range(2, slots), rest):
                rows.add((0,) * first + (1,) * second + tail)
    return sorted(rows)


def transfers(row):
    pairs = []
    for plane in range(1, len(row) // 2):
        wanted = sorted(set(row[2 * plane : 2 * plane + 2]))
        pairs += [(p // 2, plane) for p in wanted if p // 2 != plane]
    return tuple(sorted(pairs))


def key_of(row):
    as_int = lambda flag: jnp.where(flag, 1, 0) if isinstance(flag, jax.Array) else int(flag)
    key = as_int(row[2] != row[3])
    key = key + 2 * as_int(row[5] // 2 == 1) + 4 * as_int(row[5] // 2 == 3)
    key = key + 8 * as_int(row[6] // 2 == 0)
    for plane, weight in ((1, 16), (2, 48)):
        from_six = as_int(row[6] // 2 == plane)
        from_seven = as_int(row[7] // 2 == plane)
        same = as_int(row[6] == row[7])
        key = key + weight * (from_six + from_seven - from_six * same)
    return key


def plans(slots):
    found = {}
    for row in lineages(slots):
        found[key_of(row)] = transfers(row)
    out = []
    for key in sorted(found):
        rounds = []
        seen = {}
        for pair in sorted(found[key], key=lambda p: -abs(p[1] - p[0])):
            which = seen.get(pair, 0)
            seen[pair] = which + 1
            for members in rounds:
                if all(pair[0] != m[0] and pair[1] != m[1] for m in members):
                    members.append(pair + (which,))
                    break
            else:
                rounds.append([pair + (which,)])
        out.append((key, rounds))
    return out


def pack_kernel(counts, vq, vk, vv, tq, tk, tv, out, facts, *, keys):
    @pl.when(pl.program_id(0) == 0)
    def _():
        slots = counts.shape[0]
        running = [counts[0]]
        for i in range(1, slots):
            running.append(running[-1] + counts[i])
        row = [sum(jnp.where(r <= j, 1, 0) for r in running) for j in range(slots)]
        facts[0] = lax.axis_index("dom")
        for j in range(slots):
            facts[1 + j] = row[j]
        key = key_of(row)
        facts[1 + slots] = sum(jnp.where(key == k, i, 0) for i, k in enumerate(keys))

    rows, text = vq.shape[1], tq.shape[1]
    base = 3 * rows
    for p in range(vq.shape[0]):
        for h in range(vq.shape[2] // HD):
            columns = slice(h * HD, (h + 1) * HD)
            for i, ref in enumerate((vq, vk, vv)):
                out[p, h, i * rows : (i + 1) * rows, :] = ref[p, :, columns]
            for i, ref in enumerate((tq, tk, tv)):
                out[p, h, base + i * text : base + (i + 1) * text, :] = ref[p, :, columns]


def pack(counts, vq, vk, vv, tq, tk, tv, keys, steps=2):
    resident, rows, features = vq.shape
    text = tq.shape[1]
    heads = features // HD
    width = features // steps
    total = 3 * (rows + text)
    video = pl.BlockSpec((resident, rows, width), lambda i: (0, 0, i))
    words = pl.BlockSpec((resident, text, width), lambda i: (0, 0, i))
    scalars = pl.BlockSpec(memory_space=pltpu.SMEM)
    packed, facts = pl.pallas_call(
        functools.partial(pack_kernel, keys=keys),
        grid=(steps,),
        in_specs=[scalars] + [video] * 3 + [words] * 3,
        out_specs=[
            pl.BlockSpec((resident, heads // steps, total, HD), lambda i: (0, i, 0, 0)),
            scalars,
        ],
        out_shape=[
            jax.ShapeDtypeStruct((resident, heads, total, HD), vq.dtype),
            jax.ShapeDtypeStruct((counts.shape[0] + 2,), jnp.int32),
        ],
        name="pack",
    )(counts, vq, vk, vv, tq, tk, tv)
    return packed.reshape(resident * heads, total, HD), facts


def attend_kernel(x, out, k, v, *, rows, text, peers):
    n = x.shape[0]
    video_rows, text_rows = n * rows, n * text
    total = video_rows + text_rows
    base = 3 * rows
    for i, ref in ((1, k), (2, v)):
        ref[0:video_rows, 0:HD] = x[:, i * rows : (i + 1) * rows, :].reshape(video_rows, HD)
        ref[video_rows:total, 0:HD] = x[:, base + i * text : base + (i + 1) * text, :].reshape(
            text_rows, HD
        )
    v[:, HD : 2 * HD] = jnp.ones((total, HD), v.dtype)
    scale = HD**-0.5 * LOG2E

    blocks = [(i, i + peers, 0, 0, rows) for i in range(0, n, peers)] + [(0, n, base, rows, text)]

    def scored(block):
        first, last, source, _, count = block
        piece = x[first:last, source : source + count, :].reshape((last - first) * count, HD)
        return lax.dot_general(
            piece, k[...], (((1,), (1,)), ((), ())), preferred_element_type=jnp.float32
        )

    scores = scored(blocks[0])
    for i, (first, last, _, to, count) in enumerate(blocks):
        ahead = scored(blocks[i + 1]) if i + 1 < len(blocks) else None
        row_max = jnp.max(scores, axis=1, keepdims=True)
        weights = jnp.exp2((scores - row_max) * scale).astype(v.dtype)
        summed = jnp.dot(weights, v[...], preferred_element_type=jnp.float32)
        rounded = (summed[:, :HD] / summed[:, HD:]).astype(out.dtype)
        out[first:last, to : to + count, :] = rounded.reshape(last - first, count, HD)
        scores = ahead


def attend(x, rows, text, peers=8):
    n = x.shape[0]
    total = n * (rows + text)
    return pl.pallas_call(
        functools.partial(attend_kernel, rows=rows, text=text, peers=peers),
        in_specs=[pl.BlockSpec(memory_space=pltpu.VMEM)],
        out_specs=pl.BlockSpec(memory_space=pltpu.VMEM),
        out_shape=jax.ShapeDtypeStruct((n, rows + text, HD), x.dtype),
        scratch_shapes=[
            pltpu.VMEM((total, HD), x.dtype),
            pltpu.VMEM((total, 2 * HD), x.dtype),
        ],
        compiler_params=pltpu.CompilerParams(vmem_limit_bytes=VMEM_LIMIT),
        name="attend",
    )(x)


def outgoing_kernel(facts, own, *sends, rounds):
    dom = facts[0]
    for members, send in zip(rounds, sends):
        index = 0
        for source, target, which in members:
            slot = 1 + 2 * target
            if which == 0:
                wanted = jnp.where(facts[slot] // 2 == source, facts[slot], facts[slot + 1])
            else:
                wanted = facts[slot + 1]
            index = jnp.where(dom == source, lax.rem(wanted, 2), index)
        send[...] = own[index]


def outgoing(facts, own, rounds):
    vmem = pl.BlockSpec(memory_space=pltpu.VMEM)
    block = jax.ShapeDtypeStruct(own.shape[1:], own.dtype)
    return pl.pallas_call(
        functools.partial(outgoing_kernel, rounds=rounds),
        in_specs=[pl.BlockSpec(memory_space=pltpu.SMEM), vmem],
        out_specs=[vmem] * len(rounds),
        out_shape=[block] * len(rounds),
        compiler_params=pltpu.CompilerParams(vmem_limit_bytes=SMALL),
        name="outgoing",
    )(facts, own)


def finish_kernel(facts, own, *refs, rounds):
    received, (noise, video, words) = refs[:-3], refs[-3:]
    slots, rows = noise.shape[0], noise.shape[1]
    text = words.shape[1]
    dom = facts[0]
    for s in range(slots):
        ancestor = facts[1 + 2 * dom + s]
        origin = ancestor // 2
        chosen = 0
        for r, members in enumerate(rounds):
            for source, target, which in members:
                twice = sum(m[:2] == (source, target) for ms in rounds for m in ms) == 2
                if not twice or which == s:
                    hit = jnp.logical_and(dom == target, origin == source)
                    chosen = jnp.where(hit, 1 + r, chosen)

        def write(block, s=s):
            for h in range(own.shape[1]):
                columns = slice(h * HD, (h + 1) * HD)
                part = block[h, 0:rows, :].astype(jnp.float32)
                total = part + noise[s, :, columns].astype(jnp.float32)
                video[s, :, columns] = total.astype(video.dtype)
                words[s, :, columns] = block[h, rows : rows + text, :]

        @pl.when(chosen == 0)
        def _(write=write, ancestor=ancestor):
            write(own.at[lax.rem(ancestor, 2)])

        for r, block in enumerate(received):

            @pl.when(chosen == 1 + r)
            def _(write=write, block=block):
                write(block)


def finish(facts, own, received, noise, text, rounds):
    slots, _, features = noise.shape
    vmem = pl.BlockSpec(memory_space=pltpu.VMEM)
    return pl.pallas_call(
        functools.partial(finish_kernel, rounds=rounds),
        in_specs=[pl.BlockSpec(memory_space=pltpu.SMEM)] + [vmem] * (2 + len(received)),
        out_specs=[vmem, vmem],
        out_shape=[
            jax.ShapeDtypeStruct(noise.shape, noise.dtype),
            jax.ShapeDtypeStruct((slots, text, features), noise.dtype),
        ],
        compiler_params=pltpu.CompilerParams(vmem_limit_bytes=SMALL),
        name="finish",
    )(facts, own, *received, noise)


def resample(rounds, text, facts, own, noise):
    sends = outgoing(facts, own, rounds)
    received = [
        lax.ppermute(send, "dom", [m[:2] for m in members]) for send, members in zip(sends, rounds)
    ]
    return tuple(finish(facts, own, received, noise, text, rounds))


def per_device(
    counts, video_query, video_key, video_value, text_query, text_key, text_value, fresh_noise
):
    resident, rows, features = video_query.shape
    text = text_query.shape[1]
    heads = features // HD
    known = plans(counts.shape[0])

    packed, facts = pack(
        counts,
        video_query,
        video_key,
        video_value,
        text_query,
        text_key,
        text_value,
        [key for key, _ in known],
    )
    gathered = lax.all_to_all(packed, "seq", split_axis=0, concat_axis=0, tiled=True)
    attended = attend(gathered, rows, text)
    returned = lax.all_to_all(attended, "seq", split_axis=0, concat_axis=0, tiled=True)
    own = returned.reshape(resident, heads, rows + text, HD)
    branches = [functools.partial(resample, rounds, text) for _, rounds in known]
    return lax.switch(facts[counts.shape[0] + 1], branches, facts, own, fresh_noise)


def solution(mesh):
    placed = P(("rep", "dom"), "seq", None)
    return jax.shard_map(
        per_device,
        mesh=mesh,
        in_specs=(P("rep"),) + (placed,) * 7,
        out_specs=(placed, placed),
        check_vma=False,
    )
```

```python
import functools
import itertools

import jax
import jax.numpy as jnp
from jax import lax
from jax.experimental import pallas as pl
from jax.experimental.pallas import tpu as pltpu
from jax.sharding import PartitionSpec as P

HD = 128
LOG2E = 1.4426950408889634
VMEM_LIMIT = 32 * 2**20
SMALL = 16 * 2**20


def lineages(slots):
    half = slots // 2
    rows = set()
    for other in range(1, half + 1):
        for first, second in ((half, other), (other, half)):
            rest = slots - first - second
            for tail in itertools.combinations_with_replacement(range(2, slots), rest):
                rows.add((0,) * first + (1,) * second + tail)
    return sorted(rows)


def transfers(row):
    moves, relays = [], []
    planes = len(row) // 2
    for plane in range(1, planes):
        for slot in (2 * plane, 2 * plane + 1):
            home = row[slot] // 2
            if home == plane or (slot % 2 and row[slot] == row[slot - 1]):
                continue
            neighbours = [t for t in (slot // 2 * 2 - 2, slot // 2 * 2 - 1) if row[t] == row[slot]]
            if plane == planes - 1 and home < plane - 1 and neighbours:
                relays.append((slot, neighbours[0]))
            else:
                moves.append((home, plane, slot))
    return tuple(moves), tuple(relays)


def key_of(row):
    as_int = lambda flag: jnp.where(flag, 1, 0) if isinstance(flag, jax.Array) else int(flag)
    key = as_int(row[2] != row[3])
    key = key + 2 * as_int(row[5] // 2 == 1) + 4 * as_int(row[5] // 2 == 3)
    key = key + 8 * as_int(row[6] // 2 == 0)
    for plane, weight in ((1, 16), (2, 48)):
        from_six = as_int(row[6] // 2 == plane)
        from_seven = as_int(row[7] // 2 == plane)
        same = as_int(row[6] == row[7])
        key = key + weight * (from_six + from_seven - from_six * same)
    return key + 144 * as_int(row[5] // 2 == 1) * as_int(row[5] == row[6])


def links(move):
    return set(range(min(move[:2]), max(move[:2])))


def arrange(moves, relays):
    fed = {t for _, t in relays}
    order = sorted(moves, key=lambda m: (m[2] not in fed, -abs(m[1] - m[0])))
    rounds = []
    for move in order:
        for i, members in enumerate(rounds):
            apart = all(move[0] != m[0] and move[1] != m[1] for m in members)
            clear = not any(m[2] in fed and links(m) & links(move) for m in members)
            if apart and clear:
                members.append(move)
                break
        else:
            rounds.append([move])
    return rounds


def plans(slots):
    found = {}
    for row in lineages(slots):
        found[key_of(row)] = transfers(row)
    return [(key, arrange(*found[key]), found[key][1]) for key in sorted(found)]


def pack_kernel(*refs, pieces):
    arrays, out, held, sems = refs[:6], refs[6], refs[7:13], refs[13]
    width = arrays[0].shape[2] // pieces

    def copies(piece):
        columns = pl.ds(piece * width, width)
        return [
            pltpu.make_async_copy(ref.at[:, :, columns], to.at[:, :, columns], sems.at[piece, i])
            for i, (ref, to) in enumerate(zip(arrays, held))
        ]

    for piece in range(pieces):
        for copy in copies(piece):
            copy.start()
    for piece in range(pieces):
        for copy in copies(piece):
            copy.wait()
        for p in range(out.shape[0]):
            for h in range(piece * width // HD, (piece + 1) * width // HD):
                at = 0
                for ref in held:
                    out[p, h, at : at + ref.shape[1], :] = ref[p, :, h * HD : (h + 1) * HD]
                    at += ref.shape[1]


def pack(arrays, pieces=4):
    resident, rows, features = arrays[0].shape
    text = arrays[3].shape[1]
    shape = (resident, features // HD, 3 * (rows + text), HD)
    packed = pl.pallas_call(
        functools.partial(pack_kernel, pieces=pieces),
        in_specs=[pl.BlockSpec(memory_space=pl.ANY)] * 6,
        out_specs=pl.BlockSpec(memory_space=pltpu.VMEM),
        out_shape=jax.ShapeDtypeStruct(shape, arrays[0].dtype),
        scratch_shapes=[pltpu.VMEM(a.shape, a.dtype) for a in arrays]
        + [pltpu.SemaphoreType.DMA((pieces, 6))],
        compiler_params=pltpu.CompilerParams(vmem_limit_bytes=SMALL),
        name="pack",
    )(*[pltpu.with_memory_space_constraint(a, pltpu.HBM) for a in arrays])
    return packed.reshape((-1,) + shape[2:])


def facts_kernel(counts, _, facts, *, keys):
    slots = counts.shape[0]
    running = [counts[0]]
    for i in range(1, slots):
        running.append(running[-1] + counts[i])
    row = [sum(jnp.where(r <= j, 1, 0) for r in running) for j in range(slots)]
    facts[0] = lax.axis_index("dom")
    for j in range(slots):
        facts[1 + j] = row[j]
    key = key_of(row)
    facts[1 + slots] = sum(jnp.where(key == k, i, 0) for i, k in enumerate(keys))


def find_facts(counts, after, keys):
    scalars = pl.BlockSpec(memory_space=pltpu.SMEM)
    return pl.pallas_call(
        functools.partial(facts_kernel, keys=keys),
        in_specs=[scalars, pl.BlockSpec(memory_space=pl.ANY)],
        out_specs=scalars,
        out_shape=jax.ShapeDtypeStruct((counts.shape[0] + 2,), jnp.int32),
        name="facts",
    )(counts, after)


def attend_kernel(x, out, k, v, *, rows, text, peers):
    n = x.shape[0]
    video_rows, text_rows = n * rows, n * text
    total = video_rows + text_rows
    base = 3 * rows
    for i, ref in ((1, k), (2, v)):
        ref[0:video_rows, 0:HD] = x[:, i * rows : (i + 1) * rows, :].reshape(video_rows, HD)
        ref[video_rows:total, 0:HD] = x[:, base + i * text : base + (i + 1) * text, :].reshape(
            text_rows, HD
        )
    v[:, HD : 2 * HD] = jnp.ones((total, HD), v.dtype)
    scale = HD**-0.5 * LOG2E

    blocks = [(i, i + peers, 0, 0, rows) for i in range(0, n, peers)] + [(0, n, base, rows, text)]

    def scored(block):
        first, last, source, _, count = block
        piece = x[first:last, source : source + count, :].reshape((last - first) * count, HD)
        return lax.dot_general(
            piece, k[...], (((1,), (1,)), ((), ())), preferred_element_type=jnp.float32
        )

    scores = scored(blocks[0])
    for i, (first, last, _, to, count) in enumerate(blocks):
        ahead = scored(blocks[i + 1]) if i + 1 < len(blocks) else None
        row_max = jnp.max(scores, axis=1, keepdims=True)
        weights = jnp.exp2((scores - row_max) * scale).astype(v.dtype)
        summed = jnp.dot(weights, v[...], preferred_element_type=jnp.float32)
        rounded = (summed[:, :HD] / summed[:, HD:]).astype(out.dtype)
        out[first:last, to : to + count, :] = rounded.reshape(last - first, count, HD)
        scores = ahead


def attend(x, rows, text, peers=8):
    n = x.shape[0]
    total = n * (rows + text)
    return pl.pallas_call(
        functools.partial(attend_kernel, rows=rows, text=text, peers=peers),
        in_specs=[pl.BlockSpec(memory_space=pltpu.VMEM)],
        out_specs=pl.BlockSpec(memory_space=pltpu.VMEM),
        out_shape=jax.ShapeDtypeStruct((n, rows + text, HD), x.dtype),
        scratch_shapes=[
            pltpu.VMEM((total, HD), x.dtype),
            pltpu.VMEM((total, 2 * HD), x.dtype),
        ],
        compiler_params=pltpu.CompilerParams(vmem_limit_bytes=VMEM_LIMIT),
        name="attend",
    )(x)


def outgoing_kernel(facts, own, *sends, rounds):
    dom = facts[0]
    for members, send in zip(rounds, sends):
        index = 0
        for source, _, slot in members:
            index = jnp.where(dom == source, lax.rem(facts[1 + slot], 2), index)
        send[...] = own[index]


def outgoing(facts, own, rounds):
    vmem = pl.BlockSpec(memory_space=pltpu.VMEM)
    block = jax.ShapeDtypeStruct(own.shape[1:], own.dtype)
    return pl.pallas_call(
        functools.partial(outgoing_kernel, rounds=rounds),
        in_specs=[pl.BlockSpec(memory_space=pltpu.SMEM), vmem],
        out_specs=[vmem] * len(rounds),
        out_shape=[block] * len(rounds),
        compiler_params=pltpu.CompilerParams(vmem_limit_bytes=SMALL),
        name="outgoing",
    )(facts, own)


def finish_kernel(facts, own, *refs, places):
    received, (noise, video, words) = refs[:-3], refs[-3:]
    slots, rows = noise.shape[0], noise.shape[1]
    text = words.shape[1]
    dom = facts[0]
    chosen = 0
    for s in range(slots):
        ancestor = facts[1 + slots * dom + s]
        before = chosen
        chosen = 0
        for slot, r in places:
            if slot % slots == s:
                chosen = jnp.where(dom == slot // slots, 1 + r, chosen)
        if s:
            chosen = jnp.where(ancestor == facts[slots * dom + s], before, chosen)
        chosen = jnp.where(ancestor // slots == dom, 0, chosen)

        def write(block, s=s):
            for h in range(own.shape[1]):
                columns = slice(h * HD, (h + 1) * HD)
                part = block[h, 0:rows, :].astype(jnp.float32)
                total = part + noise[s, :, columns].astype(jnp.float32)
                video[s, :, columns] = total.astype(video.dtype)
                words[s, :, columns] = block[h, rows : rows + text, :]

        @pl.when(chosen == 0)
        def _(write=write, ancestor=ancestor):
            write(own.at[lax.rem(ancestor, slots)])

        for r, block in enumerate(received):

            @pl.when(chosen == 1 + r)
            def _(write=write, block=block):
                write(block)


def finish(facts, own, received, noise, text, places):
    slots, _, features = noise.shape
    vmem = pl.BlockSpec(memory_space=pltpu.VMEM)
    return pl.pallas_call(
        functools.partial(finish_kernel, places=places),
        in_specs=[pl.BlockSpec(memory_space=pltpu.SMEM)] + [vmem] * (2 + len(received)),
        out_specs=[vmem, vmem],
        out_shape=[
            jax.ShapeDtypeStruct(noise.shape, noise.dtype),
            jax.ShapeDtypeStruct((slots, text, features), noise.dtype),
        ],
        compiler_params=pltpu.CompilerParams(vmem_limit_bytes=SMALL),
        name="finish",
    )(facts, own, *received, noise)


def resample(rounds, relays, text, facts, own, noise):
    sends = outgoing(facts, own, rounds)
    received = [
        lax.ppermute(send, "dom", [m[:2] for m in members]) for send, members in zip(sends, rounds)
    ]
    places = [(m[2], r) for r, members in enumerate(rounds) for m in members]
    held = dict(places)
    for slot, neighbour in relays:
        places.append((slot, len(received)))
        hop = (neighbour // 2, slot // 2)
        received.append(lax.ppermute(received[held[neighbour]], "dom", [hop]))
    return tuple(finish(facts, own, received, noise, text, places))


def per_device(
    counts, video_query, video_key, video_value, text_query, text_key, text_value, fresh_noise
):
    resident, rows, features = video_query.shape
    text = text_query.shape[1]
    heads = features // HD
    known = plans(counts.shape[0])

    packed = pack(
        (video_query, video_key, video_value, text_query, text_key, text_value)
    )
    gathered = lax.all_to_all(packed, "seq", split_axis=0, concat_axis=0, tiled=True)
    attended = attend(gathered, rows, text)
    facts = find_facts(counts, attended, [plan[0] for plan in known])
    returned = lax.all_to_all(attended, "seq", split_axis=0, concat_axis=0, tiled=True)
    own = returned.reshape(resident, heads, rows + text, HD)
    branches = [functools.partial(resample, *plan[1:], text) for plan in known]
    return lax.switch(facts[counts.shape[0] + 1], branches, facts, own, fresh_noise)


def solution(mesh):
    placed = P(("rep", "dom"), "seq", None)
    return jax.shard_map(
        per_device,
        mesh=mesh,
        in_specs=(P("rep"),) + (placed,) * 7,
        out_specs=(placed, placed),
        check_vma=False,
    )
```

```python
import functools
import itertools

import jax
import jax.numpy as jnp
from jax import lax
from jax.experimental import pallas as pl
from jax.experimental.pallas import tpu as pltpu
from jax.sharding import PartitionSpec as P

HD = 128
LOG2E = 1.4426950408889634
VMEM_LIMIT = 32 * 2**20
SMALL = 16 * 2**20


def lineages(slots):
    half = slots // 2
    rows = set()
    for other in range(1, half + 1):
        for first, second in ((half, other), (other, half)):
            rest = slots - first - second
            for tail in itertools.combinations_with_replacement(range(2, slots), rest):
                rows.add((0,) * first + (1,) * second + tail)
    return sorted(rows)


def transfers(row):
    moves, relays = [], []
    planes = len(row) // 2
    last = planes - 1
    both = row[-2] // 2 == row[-1] // 2 and row[-2] != row[-1]
    for plane in range(1, planes):
        for slot in (2 * plane, 2 * plane + 1):
            home = row[slot] // 2
            if home == plane or (slot % 2 and row[slot] == row[slot - 1]):
                continue
            neighbours = [t for t in (2 * last - 2, 2 * last - 1) if row[t] == row[slot]]
            if plane == last and neighbours and (home == 0 or (home == 1 and both)):
                relays.append((slot, neighbours[0]))
            else:
                moves.append((home, plane, slot))
    return tuple(moves), tuple(relays)


def key_of(row):
    as_int = lambda flag: jnp.where(flag, 1, 0) if isinstance(flag, jax.Array) else int(flag)
    key = as_int(row[2] != row[3])
    key = key + 2 * as_int(row[5] // 2 == 1) + 4 * as_int(row[5] // 2 == 3)
    key = key + 8 * as_int(row[6] // 2 == 0)
    for plane, weight in ((1, 16), (2, 48)):
        from_six = as_int(row[6] // 2 == plane)
        from_seven = as_int(row[7] // 2 == plane)
        same = as_int(row[6] == row[7])
        key = key + weight * (from_six + from_seven - from_six * same)
    shared = as_int(row[5] // 2 == 1) * as_int(row[5] == row[6])
    return key + 144 * shared * as_int(row[6] != row[7]) * as_int(row[7] // 2 == 1)


def links(move):
    return set(range(min(move[:2]), max(move[:2])))


def arrange(moves, relays):
    fed = {t for _, t in relays}
    for count in range(1, len(moves) + 1):
        best = None
        for numbers in itertools.product(range(count), repeat=len(moves)):
            rounds = [[m for m, i in zip(moves, numbers) if i == r] for r in range(count)]
            if any(len({m[end] for m in ms}) < len(ms) for ms in rounds for end in (0, 1)):
                continue
            if not fed <= {m[2] for m in rounds[0]}:
                continue
            loads = [[sum(k in links(m) for m in ms) for k in range(8)] for ms in rounds]
            if any(loads[0][k] > 1 for m in rounds[0] if m[2] in fed for k in links(m)):
                continue
            early = sum(i * (4 - len(links(m))) for m, i in zip(moves, numbers))
            rank = (sum(max(load) for load in loads), early, numbers)
            if best is None or rank < best[0]:
                best = (rank, rounds)
        if best is not None:
            return best[1]
    return []


def plans(slots):
    found = {}
    for row in lineages(slots):
        found[key_of(row)] = transfers(row)
    return [(key, arrange(*found[key]), found[key][1]) for key in sorted(found)]


def pack_kernel(*refs, pieces):
    arrays, out, held, sems = refs[:6], refs[6], refs[7:13], refs[13]
    width = arrays[0].shape[2] // pieces

    def copies(piece):
        columns = pl.ds(piece * width, width)
        return [
            pltpu.make_async_copy(ref.at[:, :, columns], to.at[:, :, columns], sems.at[piece, i])
            for i, (ref, to) in enumerate(zip(arrays, held))
        ]

    for piece in range(pieces):
        for copy in copies(piece):
            copy.start()
    for piece in range(pieces):
        for copy in copies(piece):
            copy.wait()
        for p in range(out.shape[0]):
            for h in range(piece * width // HD, (piece + 1) * width // HD):
                at = 0
                for ref in held:
                    out[p, h, at : at + ref.shape[1], :] = ref[p, :, h * HD : (h + 1) * HD]
                    at += ref.shape[1]


def pack(arrays, pieces=1):
    resident, rows, features = arrays[0].shape
    text = arrays[3].shape[1]
    shape = (resident, features // HD, 3 * (rows + text), HD)
    packed = pl.pallas_call(
        functools.partial(pack_kernel, pieces=pieces),
        in_specs=[pl.BlockSpec(memory_space=pl.ANY)] * 6,
        out_specs=pl.BlockSpec(memory_space=pltpu.VMEM),
        out_shape=jax.ShapeDtypeStruct(shape, arrays[0].dtype),
        scratch_shapes=[pltpu.VMEM(a.shape, a.dtype) for a in arrays]
        + [pltpu.SemaphoreType.DMA((pieces, 6))],
        compiler_params=pltpu.CompilerParams(vmem_limit_bytes=SMALL),
        name="pack",
    )(*[pltpu.with_memory_space_constraint(a, pltpu.HBM) for a in arrays])
    return packed.reshape((-1,) + shape[2:])


def facts_kernel(counts, _, facts, *, keys):
    slots = counts.shape[0]
    running = [counts[0]]
    for i in range(1, slots):
        running.append(running[-1] + counts[i])
    row = [sum(jnp.where(r <= j, 1, 0) for r in running) for j in range(slots)]
    facts[0] = lax.axis_index("dom")
    for j in range(slots):
        facts[1 + j] = row[j]
    key = key_of(row)
    facts[1 + slots] = sum(jnp.where(key == k, i, 0) for i, k in enumerate(keys))


def find_facts(counts, after, keys):
    scalars = pl.BlockSpec(memory_space=pltpu.SMEM)
    return pl.pallas_call(
        functools.partial(facts_kernel, keys=keys),
        in_specs=[scalars, pl.BlockSpec(memory_space=pl.ANY)],
        out_specs=scalars,
        out_shape=jax.ShapeDtypeStruct((counts.shape[0] + 2,), jnp.int32),
        name="facts",
    )(counts, after)


def attend_kernel(x, out, k, v, *, rows, text, peers):
    n = x.shape[0]
    video_rows, text_rows = n * rows, n * text
    total = video_rows + text_rows
    base = 3 * rows
    for i, ref in ((1, k), (2, v)):
        ref[0:video_rows, 0:HD] = x[:, i * rows : (i + 1) * rows, :].reshape(video_rows, HD)
        ref[video_rows:total, 0:HD] = x[:, base + i * text : base + (i + 1) * text, :].reshape(
            text_rows, HD
        )
    v[:, HD : 2 * HD] = jnp.ones((total, HD), v.dtype)
    scale = HD**-0.5 * LOG2E

    blocks = [(i, i + peers, 0, 0, rows) for i in range(0, n, peers)] + [(0, n, base, rows, text)]

    def scored(block):
        first, last, source, _, count = block
        piece = x[first:last, source : source + count, :].reshape((last - first) * count, HD)
        return lax.dot_general(
            piece, k[...], (((1,), (1,)), ((), ())), preferred_element_type=jnp.float32
        )

    scores = scored(blocks[0])
    for i, (first, last, _, to, count) in enumerate(blocks):
        ahead = scored(blocks[i + 1]) if i + 1 < len(blocks) else None
        row_max = jnp.max(scores, axis=1, keepdims=True)
        weights = jnp.exp2((scores - row_max) * scale).astype(v.dtype)
        summed = jnp.dot(weights, v[...], preferred_element_type=jnp.float32)
        rounded = (summed[:, :HD] / summed[:, HD:]).astype(out.dtype)
        out[first:last, to : to + count, :] = rounded.reshape(last - first, count, HD)
        scores = ahead


def attend(x, rows, text, peers=8):
    n = x.shape[0]
    total = n * (rows + text)
    return pl.pallas_call(
        functools.partial(attend_kernel, rows=rows, text=text, peers=peers),
        in_specs=[pl.BlockSpec(memory_space=pltpu.VMEM)],
        out_specs=pl.BlockSpec(memory_space=pltpu.VMEM),
        out_shape=jax.ShapeDtypeStruct((n, rows + text, HD), x.dtype),
        scratch_shapes=[
            pltpu.VMEM((total, HD), x.dtype),
            pltpu.VMEM((total, 2 * HD), x.dtype),
        ],
        compiler_params=pltpu.CompilerParams(vmem_limit_bytes=VMEM_LIMIT),
        name="attend",
    )(x)


def outgoing_kernel(facts, own, *sends, rounds):
    dom = facts[0]
    for members, send in zip(rounds, sends):
        index = 0
        for source, _, slot in members:
            index = jnp.where(dom == source, lax.rem(facts[1 + slot], 2), index)
        send[...] = own[index]


def outgoing(facts, own, rounds):
    vmem = pl.BlockSpec(memory_space=pltpu.VMEM)
    block = jax.ShapeDtypeStruct(own.shape[1:], own.dtype)
    return pl.pallas_call(
        functools.partial(outgoing_kernel, rounds=rounds),
        in_specs=[pl.BlockSpec(memory_space=pltpu.SMEM), vmem],
        out_specs=[vmem] * len(rounds),
        out_shape=[block] * len(rounds),
        compiler_params=pltpu.CompilerParams(vmem_limit_bytes=SMALL),
        name="outgoing",
    )(facts, own)


def finish_kernel(facts, own, *refs, places):
    received, (noise, video, words) = refs[:-3], refs[-3:]
    slots, rows = noise.shape[0], noise.shape[1]
    text = words.shape[1]
    dom = facts[0]
    chosen = 0
    for s in range(slots):
        ancestor = facts[1 + slots * dom + s]
        before = chosen
        chosen = 0
        for slot, r in places:
            if slot % slots == s:
                chosen = jnp.where(dom == slot // slots, 1 + r, chosen)
        if s:
            chosen = jnp.where(ancestor == facts[slots * dom + s], before, chosen)
        chosen = jnp.where(ancestor // slots == dom, 0, chosen)

        def write(block, s=s):
            for h in range(own.shape[1]):
                columns = slice(h * HD, (h + 1) * HD)
                part = block[h, 0:rows, :].astype(jnp.float32)
                total = part + noise[s, :, columns].astype(jnp.float32)
                video[s, :, columns] = total.astype(video.dtype)
                words[s, :, columns] = block[h, rows : rows + text, :]

        @pl.when(chosen == 0)
        def _(write=write, ancestor=ancestor):
            write(own.at[lax.rem(ancestor, slots)])

        for r, block in enumerate(received):

            @pl.when(chosen == 1 + r)
            def _(write=write, block=block):
                write(block)


def finish(facts, own, received, noise, text, places):
    slots, _, features = noise.shape
    vmem = pl.BlockSpec(memory_space=pltpu.VMEM)
    return pl.pallas_call(
        functools.partial(finish_kernel, places=places),
        in_specs=[pl.BlockSpec(memory_space=pltpu.SMEM)] + [vmem] * (2 + len(received)),
        out_specs=[vmem, vmem],
        out_shape=[
            jax.ShapeDtypeStruct(noise.shape, noise.dtype),
            jax.ShapeDtypeStruct((slots, text, features), noise.dtype),
        ],
        compiler_params=pltpu.CompilerParams(vmem_limit_bytes=SMALL),
        name="finish",
    )(facts, own, *received, noise)


def resample(rounds, relays, text, facts, own, noise):
    sends = outgoing(facts, own, rounds)
    received = [
        lax.ppermute(send, "dom", [m[:2] for m in members]) for send, members in zip(sends, rounds)
    ]
    places = [(m[2], r) for r, members in enumerate(rounds) for m in members]
    held = dict(places)
    for slot, neighbour in relays:
        places.append((slot, len(received)))
        hop = (neighbour // 2, slot // 2)
        received.append(lax.ppermute(received[held[neighbour]], "dom", [hop]))
    return tuple(finish(facts, own, received, noise, text, places))


def per_device(
    counts, video_query, video_key, video_value, text_query, text_key, text_value, fresh_noise
):
    resident, rows, features = video_query.shape
    text = text_query.shape[1]
    heads = features // HD
    known = plans(counts.shape[0])

    packed = pack(
        (video_query, video_key, video_value, text_query, text_key, text_value)
    )
    gathered = lax.all_to_all(packed, "seq", split_axis=0, concat_axis=0, tiled=True)
    attended = attend(gathered, rows, text)
    facts = find_facts(counts, attended, [plan[0] for plan in known])
    returned = lax.all_to_all(attended, "seq", split_axis=0, concat_axis=0, tiled=True)
    own = returned.reshape(resident, heads, rows + text, HD)
    branches = [functools.partial(resample, *plan[1:], text) for plan in known]
    return lax.switch(facts[counts.shape[0] + 1], branches, facts, own, fresh_noise)


def solution(mesh):
    placed = P(("rep", "dom"), "seq", None)
    return jax.shard_map(
        per_device,
        mesh=mesh,
        in_specs=(P("rep"),) + (placed,) * 7,
        out_specs=(placed, placed),
        check_vma=False,
    )
```

```python
import functools
import itertools

import jax
import jax.numpy as jnp
from jax import lax
from jax.experimental import pallas as pl
from jax.experimental.pallas import tpu as pltpu
from jax.sharding import PartitionSpec as P

HD = 128
LOG2E = 1.4426950408889634
VMEM_LIMIT = 32 * 2**20
SMALL = 16 * 2**20


def lineages(slots):
    half = slots // 2
    rows = set()
    for other in range(1, half + 1):
        for first, second in ((half, other), (other, half)):
            rest = slots - first - second
            for tail in itertools.combinations_with_replacement(range(2, slots), rest):
                rows.add((0,) * first + (1,) * second + tail)
    return sorted(rows)


def transfers(row):
    moves, relays = [], []
    planes = len(row) // 2
    last = planes - 1
    both = row[-2] // 2 == row[-1] // 2 and row[-2] != row[-1]
    for plane in range(1, planes):
        for slot in (2 * plane, 2 * plane + 1):
            home = row[slot] // 2
            if home == plane or (slot % 2 and row[slot] == row[slot - 1]):
                continue
            neighbours = [t for t in (2 * last - 2, 2 * last - 1) if row[t] == row[slot]]
            if plane == last and neighbours and (home == 0 or (home == 1 and both)):
                relays.append((slot, neighbours[0]))
            else:
                moves.append((home, plane, slot))
    return tuple(moves), tuple(relays)


def key_of(row):
    as_int = lambda flag: jnp.where(flag, 1, 0) if isinstance(flag, jax.Array) else int(flag)
    key = as_int(row[2] != row[3])
    key = key + 2 * as_int(row[5] // 2 == 1) + 4 * as_int(row[5] // 2 == 3)
    key = key + 8 * as_int(row[6] // 2 == 0)
    for plane, weight in ((1, 16), (2, 48)):
        from_six = as_int(row[6] // 2 == plane)
        from_seven = as_int(row[7] // 2 == plane)
        same = as_int(row[6] == row[7])
        key = key + weight * (from_six + from_seven - from_six * same)
    shared = as_int(row[5] // 2 == 1) * as_int(row[5] == row[6])
    return key + 144 * shared * as_int(row[6] != row[7]) * as_int(row[7] // 2 == 1)


def links(move):
    return set(range(min(move[:2]), max(move[:2])))


def arrange(moves, relays):
    fed = {t for _, t in relays}
    for count in range(1, len(moves) + 1):
        best = None
        for numbers in itertools.product(range(count), repeat=len(moves)):
            rounds = [[m for m, i in zip(moves, numbers) if i == r] for r in range(count)]
            if any(len({m[end] for m in ms}) < len(ms) for ms in rounds for end in (0, 1)):
                continue
            if not fed <= {m[2] for m in rounds[0]}:
                continue
            loads = [[sum(k in links(m) for m in ms) for k in range(8)] for ms in rounds]
            if any(loads[0][k] > 1 for m in rounds[0] if m[2] in fed for k in links(m)):
                continue
            early = sum(i * (4 - len(links(m))) for m, i in zip(moves, numbers))
            rank = (sum(max(load) for load in loads), early, numbers)
            if best is None or rank < best[0]:
                best = (rank, rounds)
        if best is not None:
            return best[1]
    return []


def plans(slots):
    found = {}
    for row in lineages(slots):
        found[key_of(row)] = transfers(row)
    return [(key, arrange(*found[key]), found[key][1]) for key in sorted(found)]


def pack_kernel(*refs):
    arrays, out = refs[:-1], refs[-1]
    for p in range(out.shape[0]):
        for h in range(out.shape[1]):
            at = 0
            for ref in arrays:
                out[p, h, at : at + ref.shape[1], :] = ref[p, :, h * HD : (h + 1) * HD]
                at += ref.shape[1]


def pack(arrays):
    resident, rows, features = arrays[0].shape
    text = arrays[3].shape[1]
    shape = (resident, features // HD, 3 * (rows + text), HD)
    packed = pl.pallas_call(
        pack_kernel,
        grid=(1,),
        in_specs=[pl.BlockSpec(a.shape, lambda i: (0, 0, 0)) for a in arrays],
        out_specs=pl.BlockSpec(memory_space=pltpu.VMEM),
        out_shape=jax.ShapeDtypeStruct(shape, arrays[0].dtype),
        compiler_params=pltpu.CompilerParams(vmem_limit_bytes=SMALL),
        name="pack",
    )(*[pltpu.with_memory_space_constraint(a, pltpu.HBM) for a in arrays])
    return packed.reshape((-1,) + shape[2:])


def facts_kernel(counts, _, facts, *, keys):
    slots = counts.shape[0]
    running = [counts[0]]
    for i in range(1, slots):
        running.append(running[-1] + counts[i])
    row = [sum(jnp.where(r <= j, 1, 0) for r in running) for j in range(slots)]
    facts[0] = lax.axis_index("dom")
    for j in range(slots):
        facts[1 + j] = row[j]
    key = key_of(row)
    facts[1 + slots] = sum(jnp.where(key == k, i, 0) for i, k in enumerate(keys))


def find_facts(counts, after, keys):
    scalars = pl.BlockSpec(memory_space=pltpu.SMEM)
    return pl.pallas_call(
        functools.partial(facts_kernel, keys=keys),
        in_specs=[scalars, pl.BlockSpec(memory_space=pl.ANY)],
        out_specs=scalars,
        out_shape=jax.ShapeDtypeStruct((counts.shape[0] + 2,), jnp.int32),
        name="facts",
    )(counts, after)


def attend_kernel(x, out, k, v, *, rows, text, peers):
    n = x.shape[0]
    video_rows, text_rows = n * rows, n * text
    total = video_rows + text_rows
    base = 3 * rows
    for i, ref in ((1, k), (2, v)):
        ref[0:video_rows, 0:HD] = x[:, i * rows : (i + 1) * rows, :].reshape(video_rows, HD)
        ref[video_rows:total, 0:HD] = x[:, base + i * text : base + (i + 1) * text, :].reshape(
            text_rows, HD
        )
    v[:, HD : 2 * HD] = jnp.ones((total, HD), v.dtype)
    scale = HD**-0.5 * LOG2E

    blocks = [(i, i + peers, 0, 0, rows) for i in range(0, n, peers)] + [(0, n, base, rows, text)]

    def scored(block):
        first, last, source, _, count = block
        piece = x[first:last, source : source + count, :].reshape((last - first) * count, HD)
        return lax.dot_general(
            piece, k[...], (((1,), (1,)), ((), ())), preferred_element_type=jnp.float32
        )

    scores = scored(blocks[0])
    for i, (first, last, _, to, count) in enumerate(blocks):
        ahead = scored(blocks[i + 1]) if i + 1 < len(blocks) else None
        row_max = jnp.max(scores, axis=1, keepdims=True)
        weights = jnp.exp2((scores - row_max) * scale).astype(v.dtype)
        summed = jnp.dot(weights, v[...], preferred_element_type=jnp.float32)
        rounded = (summed[:, :HD] / summed[:, HD:]).astype(out.dtype)
        out[first:last, to : to + count, :] = rounded.reshape(last - first, count, HD)
        scores = ahead


def attend(x, rows, text, peers=8):
    n = x.shape[0]
    total = n * (rows + text)
    return pl.pallas_call(
        functools.partial(attend_kernel, rows=rows, text=text, peers=peers),
        in_specs=[pl.BlockSpec(memory_space=pltpu.VMEM)],
        out_specs=pl.BlockSpec(memory_space=pltpu.VMEM),
        out_shape=jax.ShapeDtypeStruct((n, rows + text, HD), x.dtype),
        scratch_shapes=[
            pltpu.VMEM((total, HD), x.dtype),
            pltpu.VMEM((total, 2 * HD), x.dtype),
        ],
        compiler_params=pltpu.CompilerParams(vmem_limit_bytes=VMEM_LIMIT),
        name="attend",
    )(x)


def outgoing_kernel(facts, own, *sends, rounds):
    dom = facts[0]
    for members, send in zip(rounds, sends):
        index = 0
        for source, _, slot in members:
            index = jnp.where(dom == source, lax.rem(facts[1 + slot], 2), index)
        send[...] = own[index]


def outgoing(facts, own, rounds):
    vmem = pl.BlockSpec(memory_space=pltpu.VMEM)
    block = jax.ShapeDtypeStruct(own.shape[1:], own.dtype)
    return pl.pallas_call(
        functools.partial(outgoing_kernel, rounds=rounds),
        in_specs=[pl.BlockSpec(memory_space=pltpu.SMEM), vmem],
        out_specs=[vmem] * len(rounds),
        out_shape=[block] * len(rounds),
        compiler_params=pltpu.CompilerParams(vmem_limit_bytes=SMALL),
        name="outgoing",
    )(facts, own)


def finish_kernel(facts, own, *refs, places):
    received, (noise, video, words) = refs[:-3], refs[-3:]
    slots, rows = noise.shape[0], noise.shape[1]
    text = words.shape[1]
    dom = facts[0]
    chosen = 0
    for s in range(slots):
        ancestor = facts[1 + slots * dom + s]
        before = chosen
        chosen = 0
        for slot, r in places:
            if slot % slots == s:
                chosen = jnp.where(dom == slot // slots, 1 + r, chosen)
        if s:
            chosen = jnp.where(ancestor == facts[slots * dom + s], before, chosen)
        chosen = jnp.where(ancestor // slots == dom, 0, chosen)

        def write(block, s=s):
            for h in range(own.shape[1]):
                columns = slice(h * HD, (h + 1) * HD)
                part = block[h, 0:rows, :].astype(jnp.float32)
                total = part + noise[s, :, columns].astype(jnp.float32)
                video[s, :, columns] = total.astype(video.dtype)
                words[s, :, columns] = block[h, rows : rows + text, :]

        @pl.when(chosen == 0)
        def _(write=write, ancestor=ancestor):
            write(own.at[lax.rem(ancestor, slots)])

        for r, block in enumerate(received):

            @pl.when(chosen == 1 + r)
            def _(write=write, block=block):
                write(block)


def finish(facts, own, received, noise, text, places):
    slots, _, features = noise.shape
    vmem = pl.BlockSpec(memory_space=pltpu.VMEM)
    return pl.pallas_call(
        functools.partial(finish_kernel, places=places),
        in_specs=[pl.BlockSpec(memory_space=pltpu.SMEM)] + [vmem] * (2 + len(received)),
        out_specs=[vmem, vmem],
        out_shape=[
            jax.ShapeDtypeStruct(noise.shape, noise.dtype),
            jax.ShapeDtypeStruct((slots, text, features), noise.dtype),
        ],
        compiler_params=pltpu.CompilerParams(vmem_limit_bytes=SMALL),
        name="finish",
    )(facts, own, *received, noise)


def resample(rounds, relays, text, facts, own, noise):
    sends = outgoing(facts, own, rounds)
    received = [
        lax.ppermute(send, "dom", [m[:2] for m in members]) for send, members in zip(sends, rounds)
    ]
    places = [(m[2], r) for r, members in enumerate(rounds) for m in members]
    held = dict(places)
    for slot, neighbour in relays:
        places.append((slot, len(received)))
        hop = (neighbour // 2, slot // 2)
        received.append(lax.ppermute(received[held[neighbour]], "dom", [hop]))
    return tuple(finish(facts, own, received, noise, text, places))


def per_device(
    counts, video_query, video_key, video_value, text_query, text_key, text_value, fresh_noise
):
    resident, rows, features = video_query.shape
    text = text_query.shape[1]
    heads = features // HD
    known = plans(counts.shape[0])

    packed = pack(
        (video_query, video_key, video_value, text_query, text_key, text_value)
    )
    gathered = lax.all_to_all(packed, "seq", split_axis=0, concat_axis=0, tiled=True)
    attended = attend(gathered, rows, text)
    facts = find_facts(counts, attended, [plan[0] for plan in known])
    returned = lax.all_to_all(attended, "seq", split_axis=0, concat_axis=0, tiled=True)
    own = returned.reshape(resident, heads, rows + text, HD)
    branches = [functools.partial(resample, *plan[1:], text) for plan in known]
    return lax.switch(facts[counts.shape[0] + 1], branches, facts, own, fresh_noise)


def solution(mesh):
    placed = P(("rep", "dom"), "seq", None)
    return jax.shard_map(
        per_device,
        mesh=mesh,
        in_specs=(P("rep"),) + (placed,) * 7,
        out_specs=(placed, placed),
        check_vma=False,
    )
```

```python
import functools
import itertools

import jax
import jax.numpy as jnp
from jax import lax
from jax.experimental import pallas as pl
from jax.experimental.pallas import tpu as pltpu
from jax.sharding import PartitionSpec as P

HD = 128
LOG2E = 1.4426950408889634
VMEM_LIMIT = 32 * 2**20
SMALL = 16 * 2**20


def lineages(slots):
    half = slots // 2
    rows = set()
    for other in range(1, half + 1):
        for first, second in ((half, other), (other, half)):
            rest = slots - first - second
            for tail in itertools.combinations_with_replacement(range(2, slots), rest):
                rows.add((0,) * first + (1,) * second + tail)
    return sorted(rows)


def transfers(row):
    moves, relays = [], []
    planes = len(row) // 2
    last = planes - 1
    both = row[-2] // 2 == row[-1] // 2 and row[-2] != row[-1]
    for plane in range(1, planes):
        for slot in (2 * plane, 2 * plane + 1):
            home = row[slot] // 2
            if home == plane or (slot % 2 and row[slot] == row[slot - 1]):
                continue
            neighbours = [t for t in (2 * last - 2, 2 * last - 1) if row[t] == row[slot]]
            if plane == last and neighbours and (home == 0 or (home == 1 and both)):
                relays.append((slot, neighbours[0]))
            else:
                moves.append((home, plane, slot))
    return tuple(moves), tuple(relays)


def key_of(row):
    as_int = lambda flag: jnp.where(flag, 1, 0) if isinstance(flag, jax.Array) else int(flag)
    key = as_int(row[2] != row[3])
    key = key + 2 * as_int(row[5] // 2 == 1) + 4 * as_int(row[5] // 2 == 3)
    key = key + 8 * as_int(row[6] // 2 == 0)
    for plane, weight in ((1, 16), (2, 48)):
        from_six = as_int(row[6] // 2 == plane)
        from_seven = as_int(row[7] // 2 == plane)
        same = as_int(row[6] == row[7])
        key = key + weight * (from_six + from_seven - from_six * same)
    shared = as_int(row[5] // 2 == 1) * as_int(row[5] == row[6])
    return key + 144 * shared * as_int(row[6] != row[7]) * as_int(row[7] // 2 == 1)


def links(move):
    return set(range(min(move[:2]), max(move[:2])))


def arrange(moves, relays):
    fed = {t for _, t in relays}
    for count in range(1, len(moves) + 1):
        best = None
        for numbers in itertools.product(range(count), repeat=len(moves)):
            rounds = [[m for m, i in zip(moves, numbers) if i == r] for r in range(count)]
            if any(len({m[end] for m in ms}) < len(ms) for ms in rounds for end in (0, 1)):
                continue
            if not fed <= {m[2] for m in rounds[0]}:
                continue
            loads = [[sum(k in links(m) for m in ms) for k in range(8)] for ms in rounds]
            if any(loads[0][k] > 1 for m in rounds[0] if m[2] in fed for k in links(m)):
                continue
            early = sum(i * (4 - len(links(m))) for m, i in zip(moves, numbers))
            rank = (sum(max(load) for load in loads), early, numbers)
            if best is None or rank < best[0]:
                best = (rank, rounds)
        if best is not None:
            return best[1]
    return []


def plans(slots):
    found = {}
    for row in lineages(slots):
        found[key_of(row)] = transfers(row)
    return [(key, arrange(*found[key]), found[key][1]) for key in sorted(found)]


def pack_kernel(*refs):
    arrays, out = refs[:-1], refs[-1]
    for p in range(out.shape[0]):
        for h in range(out.shape[1]):
            at = 0
            for ref in arrays:
                out[p, h, at : at + ref.shape[1], :] = ref[p, :, h * HD : (h + 1) * HD]
                at += ref.shape[1]


def pack(arrays):
    resident, rows, features = arrays[0].shape
    text = arrays[3].shape[1]
    shape = (resident, features // HD, 3 * (rows + text), HD)
    packed = pl.pallas_call(
        pack_kernel,
        grid=(1,),
        in_specs=[pl.BlockSpec(a.shape, lambda i: (0, 0, 0)) for a in arrays],
        out_specs=pl.BlockSpec(memory_space=pltpu.VMEM),
        out_shape=jax.ShapeDtypeStruct(shape, arrays[0].dtype),
        compiler_params=pltpu.CompilerParams(vmem_limit_bytes=SMALL),
        name="pack",
    )(*[pltpu.with_memory_space_constraint(a, pltpu.HBM) for a in arrays])
    return packed.reshape((-1,) + shape[2:])


def facts_kernel(counts, _, code, plan, *, keys):
    slots = counts.shape[0]
    running = [counts[0]]
    for i in range(1, slots):
        running.append(running[-1] + counts[i])
    row = [sum(jnp.where(r <= j, 1, 0) for r in running) for j in range(slots)]
    dom = lax.axis_index("dom")
    first, second = (
        sum(jnp.where(dom == plane, row[2 * plane + s], 0) for plane in range(slots // 2))
        for s in range(2)
    )
    kind = jnp.where(first // 2 == dom, lax.rem(first, 2), 2)
    bits = dom + 4 * kind
    kind = jnp.where(first == second, 3, 2)
    kind = jnp.where(second // 2 == dom, lax.rem(second, 2), kind)
    bits = bits + 16 * kind
    for j in range(slots):
        bits = bits + lax.rem(row[j], 2) * 2 ** (6 + j)
    code[...] = jnp.full(code.shape, bits, jnp.int32)
    key = key_of(row)
    plan[0] = sum(jnp.where(key == k, i, 0) for i, k in enumerate(keys))


def find_facts(counts, after, keys):
    scalars = pl.BlockSpec(memory_space=pltpu.SMEM)
    return pl.pallas_call(
        functools.partial(facts_kernel, keys=keys),
        in_specs=[scalars, pl.BlockSpec(memory_space=pl.ANY)],
        out_specs=[pl.BlockSpec(memory_space=pltpu.VMEM), scalars],
        out_shape=[
            jax.ShapeDtypeStruct((8, HD), jnp.int32),
            jax.ShapeDtypeStruct((1,), jnp.int32),
        ],
        name="facts",
    )(counts, after)


def attend_kernel(x, out, k, v, *, rows, text, peers):
    n = x.shape[0]
    video_rows, text_rows = n * rows, n * text
    total = video_rows + text_rows
    base = 3 * rows
    for i, ref in ((1, k), (2, v)):
        ref[0:video_rows, 0:HD] = x[:, i * rows : (i + 1) * rows, :].reshape(video_rows, HD)
        ref[video_rows:total, 0:HD] = x[:, base + i * text : base + (i + 1) * text, :].reshape(
            text_rows, HD
        )
    v[:, HD : 2 * HD] = jnp.ones((total, HD), v.dtype)
    scale = HD**-0.5 * LOG2E

    blocks = [(i, i + peers, 0, 0, rows) for i in range(0, n, peers)] + [(0, n, base, rows, text)]

    def scored(block):
        first, last, source, _, count = block
        piece = x[first:last, source : source + count, :].reshape((last - first) * count, HD)
        return lax.dot_general(
            piece, k[...], (((1,), (1,)), ((), ())), preferred_element_type=jnp.float32
        )

    scores = scored(blocks[0])
    for i, (first, last, _, to, count) in enumerate(blocks):
        ahead = scored(blocks[i + 1]) if i + 1 < len(blocks) else None
        row_max = jnp.max(scores, axis=1, keepdims=True)
        weights = jnp.exp2((scores - row_max) * scale).astype(v.dtype)
        summed = jnp.dot(weights, v[...], preferred_element_type=jnp.float32)
        rounded = (summed[:, :HD] / summed[:, HD:]).astype(out.dtype)
        out[first:last, to : to + count, :] = rounded.reshape(last - first, count, HD)
        scores = ahead


def attend(x, rows, text, peers=8):
    n = x.shape[0]
    total = n * (rows + text)
    return pl.pallas_call(
        functools.partial(attend_kernel, rows=rows, text=text, peers=peers),
        in_specs=[pl.BlockSpec(memory_space=pltpu.VMEM)],
        out_specs=pl.BlockSpec(memory_space=pltpu.VMEM),
        out_shape=jax.ShapeDtypeStruct((n, rows + text, HD), x.dtype),
        scratch_shapes=[
            pltpu.VMEM((total, HD), x.dtype),
            pltpu.VMEM((total, 2 * HD), x.dtype),
        ],
        compiler_params=pltpu.CompilerParams(vmem_limit_bytes=VMEM_LIMIT),
        name="attend",
    )(x)


def outgoing_kernel(facts, own, *sends, rounds):
    bits = jnp.max(facts[...])
    dom = bits & 3
    for members, send in zip(rounds, sends):
        index = 0
        for source, _, slot in members:
            index = jnp.where(dom == source, (bits >> (6 + slot)) & 1, index)
        send[...] = own[index]


def outgoing(facts, own, rounds):
    vmem = pl.BlockSpec(memory_space=pltpu.VMEM)
    block = jax.ShapeDtypeStruct(own.shape[1:], own.dtype)
    return pl.pallas_call(
        functools.partial(outgoing_kernel, rounds=rounds),
        in_specs=[vmem, vmem],
        out_specs=[vmem] * len(rounds),
        out_shape=[block] * len(rounds),
        compiler_params=pltpu.CompilerParams(vmem_limit_bytes=SMALL),
        name="outgoing",
    )(facts, own)


def finish_kernel(facts, own, *refs, places):
    received, (noise, video, words) = refs[:-3], refs[-3:]
    slots, rows = noise.shape[0], noise.shape[1]
    text = words.shape[1]
    bits = jnp.max(facts[...])
    dom = bits & 3
    chosen = 0
    for s in range(slots):
        kind = (bits >> (2 + 2 * s)) & 3
        before = chosen
        chosen = 0
        for slot, r in places:
            if slot % slots == s:
                chosen = jnp.where(dom == slot // slots, 1 + r, chosen)
        if s:
            chosen = jnp.where(kind == 3, before, chosen)
        chosen = jnp.where(kind < 2, 0, chosen)

        def write(block, s=s):
            for h in range(own.shape[1]):
                columns = slice(h * HD, (h + 1) * HD)
                part = block[h, 0:rows, :].astype(jnp.float32)
                total = part + noise[s, :, columns].astype(jnp.float32)
                video[s, :, columns] = total.astype(video.dtype)
                words[s, :, columns] = block[h, rows : rows + text, :]

        @pl.when(chosen == 0)
        def _(write=write, kind=kind):
            write(own.at[kind & 1])

        for r, block in enumerate(received):

            @pl.when(chosen == 1 + r)
            def _(write=write, block=block):
                write(block)


def finish(facts, own, received, noise, text, places):
    slots, _, features = noise.shape
    vmem = pl.BlockSpec(memory_space=pltpu.VMEM)
    return pl.pallas_call(
        functools.partial(finish_kernel, places=places),
        in_specs=[vmem] * (3 + len(received)),
        out_specs=[vmem, vmem],
        out_shape=[
            jax.ShapeDtypeStruct(noise.shape, noise.dtype),
            jax.ShapeDtypeStruct((slots, text, features), noise.dtype),
        ],
        compiler_params=pltpu.CompilerParams(vmem_limit_bytes=SMALL),
        name="finish",
    )(facts, own, *received, noise)


def resample(rounds, relays, text, facts, own, noise):
    sends = outgoing(facts, own, rounds)
    received = [
        lax.ppermute(send, "dom", [m[:2] for m in members]) for send, members in zip(sends, rounds)
    ]
    places = [(m[2], r) for r, members in enumerate(rounds) for m in members]
    held = dict(places)
    for slot, neighbour in relays:
        places.append((slot, len(received)))
        hop = (neighbour // 2, slot // 2)
        received.append(lax.ppermute(received[held[neighbour]], "dom", [hop]))
    return tuple(finish(facts, own, received, noise, text, places))


def per_device(
    counts, video_query, video_key, video_value, text_query, text_key, text_value, fresh_noise
):
    resident, rows, features = video_query.shape
    text = text_query.shape[1]
    heads = features // HD
    known = plans(counts.shape[0])

    packed = pack(
        (video_query, video_key, video_value, text_query, text_key, text_value)
    )
    gathered = lax.all_to_all(packed, "seq", split_axis=0, concat_axis=0, tiled=True)
    attended = attend(gathered, rows, text)
    facts, plan = find_facts(counts, attended, [entry[0] for entry in known])
    returned = lax.all_to_all(attended, "seq", split_axis=0, concat_axis=0, tiled=True)
    own = returned.reshape(resident, heads, rows + text, HD)
    branches = [functools.partial(resample, *entry[1:], text) for entry in known]
    return lax.switch(plan[0], branches, facts, own, fresh_noise)


def solution(mesh):
    placed = P(("rep", "dom"), "seq", None)
    return jax.shard_map(
        per_device,
        mesh=mesh,
        in_specs=(P("rep"),) + (placed,) * 7,
        out_specs=(placed, placed),
        check_vma=False,
    )
```

```python
import functools
import itertools

import jax
import jax.numpy as jnp
from jax import lax
from jax.experimental import pallas as pl
from jax.experimental.pallas import tpu as pltpu
from jax.sharding import PartitionSpec as P

HD = 128
LOG2E = 1.4426950408889634
VMEM_LIMIT = 32 * 2**20
SMALL = 16 * 2**20


def lineages(slots):
    half = slots // 2
    rows = set()
    for other in range(1, half + 1):
        for first, second in ((half, other), (other, half)):
            rest = slots - first - second
            for tail in itertools.combinations_with_replacement(range(2, slots), rest):
                rows.add((0,) * first + (1,) * second + tail)
    return sorted(rows)


def transfers(row):
    moves, relays = [], []
    planes = len(row) // 2
    last = planes - 1
    both = row[-2] // 2 == row[-1] // 2 and row[-2] != row[-1]
    for plane in range(1, planes):
        for slot in (2 * plane, 2 * plane + 1):
            home = row[slot] // 2
            if home == plane or (slot % 2 and row[slot] == row[slot - 1]):
                continue
            neighbours = [t for t in (2 * last - 2, 2 * last - 1) if row[t] == row[slot]]
            if plane == last and neighbours and (home == 0 or (home == 1 and both)):
                relays.append((slot, neighbours[0]))
            else:
                moves.append((home, plane, slot))
    return tuple(moves), tuple(relays)


def key_of(row):
    as_int = lambda flag: jnp.where(flag, 1, 0) if isinstance(flag, jax.Array) else int(flag)
    key = as_int(row[2] != row[3])
    key = key + 2 * as_int(row[5] // 2 == 1) + 4 * as_int(row[5] // 2 == 3)
    key = key + 8 * as_int(row[6] // 2 == 0)
    for plane, weight in ((1, 16), (2, 48)):
        from_six = as_int(row[6] // 2 == plane)
        from_seven = as_int(row[7] // 2 == plane)
        same = as_int(row[6] == row[7])
        key = key + weight * (from_six + from_seven - from_six * same)
    shared = as_int(row[5] // 2 == 1) * as_int(row[5] == row[6])
    return key + 144 * shared * as_int(row[6] != row[7]) * as_int(row[7] // 2 == 1)


def links(move):
    return set(range(min(move[:2]), max(move[:2])))


def arrange(moves, relays):
    fed = {t for _, t in relays}
    for count in range(1, len(moves) + 1):
        best = None
        for numbers in itertools.product(range(count), repeat=len(moves)):
            rounds = [[m for m, i in zip(moves, numbers) if i == r] for r in range(count)]
            if any(len({m[end] for m in ms}) < len(ms) for ms in rounds for end in (0, 1)):
                continue
            if not fed <= {m[2] for m in rounds[0]}:
                continue
            loads = [[sum(k in links(m) for m in ms) for k in range(8)] for ms in rounds]
            if any(loads[0][k] > 1 for m in rounds[0] if m[2] in fed for k in links(m)):
                continue
            early = sum(i * (4 - len(links(m))) for m, i in zip(moves, numbers))
            rank = (sum(max(load) for load in loads), early, numbers)
            if best is None or rank < best[0]:
                best = (rank, rounds)
        if best is not None:
            return best[1]
    return []


def plans(slots):
    found = {}
    for row in lineages(slots):
        found[key_of(row)] = transfers(row)
    return [(key, arrange(*found[key]), found[key][1]) for key in sorted(found)]


def pack_kernel(*refs):
    arrays, out = refs[:-1], refs[-1]
    for p in range(out.shape[0]):
        for h in range(out.shape[1]):
            at = 0
            for ref in arrays:
                out[p, h, at : at + ref.shape[1], :] = ref[p, :, h * HD : (h + 1) * HD]
                at += ref.shape[1]


def pack(arrays):
    resident, rows, features = arrays[0].shape
    text = arrays[3].shape[1]
    shape = (resident, features // HD, 3 * (rows + text), HD)
    packed = pl.pallas_call(
        pack_kernel,
        grid=(1,),
        in_specs=[pl.BlockSpec(a.shape, lambda i: (0, 0, 0)) for a in arrays],
        out_specs=pl.BlockSpec(memory_space=pltpu.VMEM),
        out_shape=jax.ShapeDtypeStruct(shape, arrays[0].dtype),
        compiler_params=pltpu.CompilerParams(vmem_limit_bytes=SMALL),
        name="pack",
    )(*[pltpu.with_memory_space_constraint(a, pltpu.HBM) for a in arrays])
    return packed.reshape((-1,) + shape[2:])


def facts_kernel(counts, _, code, plan, *, keys):
    slots = counts.shape[0]
    running = [counts[0]]
    for i in range(1, slots):
        running.append(running[-1] + counts[i])
    row = [sum(jnp.where(r <= j, 1, 0) for r in running) for j in range(slots)]
    dom = lax.axis_index("dom")
    first, second = (
        sum(jnp.where(dom == plane, row[2 * plane + s], 0) for plane in range(slots // 2))
        for s in range(2)
    )
    kind = jnp.where(first // 2 == dom, lax.rem(first, 2), 2)
    bits = dom + 4 * kind
    kind = jnp.where(first == second, 3, 2)
    kind = jnp.where(second // 2 == dom, lax.rem(second, 2), kind)
    bits = bits + 16 * kind
    for j in range(slots):
        bits = bits + lax.rem(row[j], 2) * 2 ** (6 + j)
    code[...] = jnp.full(code.shape, bits, jnp.int32)
    key = key_of(row)
    plan[0] = sum(jnp.where(key == k, i, 0) for i, k in enumerate(keys))


def find_facts(counts, after, keys):
    scalars = pl.BlockSpec(memory_space=pltpu.SMEM)
    return pl.pallas_call(
        functools.partial(facts_kernel, keys=keys),
        in_specs=[scalars, pl.BlockSpec(memory_space=pl.ANY)],
        out_specs=[pl.BlockSpec(memory_space=pltpu.VMEM), scalars],
        out_shape=[
            jax.ShapeDtypeStruct((8, HD), jnp.int32),
            jax.ShapeDtypeStruct((1,), jnp.int32),
        ],
        name="facts",
    )(counts, after)


def attend_kernel(x, out, k, v, *, rows, text, peers):
    n = x.shape[0]
    video_rows, text_rows = n * rows, n * text
    total = video_rows + text_rows
    base = 3 * rows
    for i, ref in ((1, k), (2, v)):
        ref[0:video_rows, 0:HD] = x[:, i * rows : (i + 1) * rows, :].reshape(video_rows, HD)
        ref[video_rows:total, 0:HD] = x[:, base + i * text : base + (i + 1) * text, :].reshape(
            text_rows, HD
        )
    v[:, HD : 2 * HD] = jnp.ones((total, HD), v.dtype)
    scale = HD**-0.5 * LOG2E

    blocks = [(i, i + peers, 0, 0, rows) for i in range(0, n, peers)] + [(0, n, base, rows, text)]

    def scored(block):
        first, last, source, _, count = block
        piece = x[first:last, source : source + count, :].reshape((last - first) * count, HD)
        return lax.dot_general(
            piece, k[...], (((1,), (1,)), ((), ())), preferred_element_type=jnp.float32
        )

    scores = scored(blocks[0])
    for i, (first, last, _, to, count) in enumerate(blocks):
        ahead = scored(blocks[i + 1]) if i + 1 < len(blocks) else None
        row_max = jnp.max(scores, axis=1, keepdims=True)
        weights = jnp.exp2((scores - row_max) * scale).astype(v.dtype)
        summed = jnp.dot(weights, v[...], preferred_element_type=jnp.float32)
        rounded = (summed[:, :HD] / summed[:, HD:]).astype(out.dtype)
        out[first:last, to : to + count, :] = rounded.reshape(last - first, count, HD)
        scores = ahead


def attend(x, rows, text, peers=8):
    n = x.shape[0]
    total = n * (rows + text)
    return pl.pallas_call(
        functools.partial(attend_kernel, rows=rows, text=text, peers=peers),
        in_specs=[pl.BlockSpec(memory_space=pltpu.VMEM)],
        out_specs=pl.BlockSpec(memory_space=pltpu.VMEM),
        out_shape=jax.ShapeDtypeStruct((n, rows + text, HD), x.dtype),
        scratch_shapes=[
            pltpu.VMEM((total, HD), x.dtype),
            pltpu.VMEM((total, 2 * HD), x.dtype),
        ],
        compiler_params=pltpu.CompilerParams(vmem_limit_bytes=VMEM_LIMIT),
        name="attend",
    )(x)


def outgoing_kernel(facts, own, *sends, rounds):
    bits = jnp.max(facts[...])
    dom = bits & 3
    for members, send in zip(rounds, sends):
        index = 0
        for source, _, slot in members:
            index = jnp.where(dom == source, (bits >> (6 + slot)) & 1, index)
        send[...] = own[index]


def outgoing(facts, own, rounds):
    vmem = pl.BlockSpec(memory_space=pltpu.VMEM)
    block = jax.ShapeDtypeStruct(own.shape[1:], own.dtype)
    return pl.pallas_call(
        functools.partial(outgoing_kernel, rounds=rounds),
        in_specs=[vmem, vmem],
        out_specs=[vmem] * len(rounds),
        out_shape=[block] * len(rounds),
        compiler_params=pltpu.CompilerParams(vmem_limit_bytes=SMALL),
        name="outgoing",
    )(facts, own)


def finish_kernel(facts, *refs, places, count, late):
    n = 1 if late else count
    blocks, noise = refs[:n], refs[n]
    video_out, words_out, video, words, sems = refs[-5:]
    slots, rows = noise.shape[0], noise.shape[1]
    text = words.shape[1]
    bits = jnp.max(facts[...])
    dom = bits & 3
    chosen = 0
    mine = []
    for s in range(slots):
        kind = (bits >> (2 + 2 * s)) & 3
        before = chosen
        chosen = 0
        for slot, r in places:
            if slot % slots == s:
                chosen = jnp.where(dom == slot // slots, 1 + r, chosen)
        if s:
            chosen = jnp.where(kind == 3, before, chosen)
        chosen = jnp.where(kind < 2, 0, chosen)
        mine.append(chosen == count if late else chosen != count)

        def write(block, s=s):
            for h in range(block.shape[0]):
                columns = slice(h * HD, (h + 1) * HD)
                part = block[h, 0:rows, :].astype(jnp.float32)
                total = part + noise[s, :, columns].astype(jnp.float32)
                video[s, :, columns] = total.astype(video.dtype)
                words[s, :, columns] = block[h, rows : rows + text, :]

        for i, block in enumerate(blocks):

            @pl.when(chosen == (count if late else i))
            def _(write=write, block=block, kind=kind, whole=not late and i == 0):
                write(block.at[kind & 1] if whole else block)

        @pl.when(mine[s])
        def _(s=s):
            pltpu.make_async_copy(video.at[s], video_out.at[s], sems.at[s]).start()
            pltpu.make_async_copy(words.at[s], words_out.at[s], sems.at[slots + s]).start()

    for s in range(slots):

        @pl.when(mine[s])
        def _(s=s):
            pltpu.make_async_copy(video.at[s], video_out.at[s], sems.at[s]).wait()
            pltpu.make_async_copy(words.at[s], words_out.at[s], sems.at[slots + s]).wait()


def finish(facts, blocks, noise, text, places, count, done=()):
    slots, _, features = noise.shape
    vmem, anywhere = pl.BlockSpec(memory_space=pltpu.VMEM), pl.BlockSpec(memory_space=pl.ANY)
    first = 2 + len(blocks)
    shapes = [noise.shape, (slots, text, features)]
    return pl.pallas_call(
        functools.partial(finish_kernel, places=places, count=count, late=bool(done)),
        in_specs=[vmem] * first + [anywhere] * len(done),
        out_specs=[anywhere] * 2,
        out_shape=[jax.ShapeDtypeStruct(shape, noise.dtype) for shape in shapes],
        scratch_shapes=[pltpu.VMEM(shape, noise.dtype) for shape in shapes]
        + [pltpu.SemaphoreType.DMA((2 * slots,))],
        input_output_aliases={first + i: i for i in range(len(done))},
        compiler_params=pltpu.CompilerParams(vmem_limit_bytes=SMALL),
        name="finish_late" if done else "finish_early",
    )(facts, *blocks, noise, *done)


def resample(rounds, relays, text, facts, own, noise):
    sends = outgoing(facts, own, rounds)
    received = [
        lax.ppermute(send, "dom", [m[:2] for m in members]) for send, members in zip(sends, rounds)
    ]
    places = [(m[2], r) for r, members in enumerate(rounds) for m in members]
    held = dict(places)
    for slot, neighbour in relays:
        places.append((slot, len(received)))
        hop = (neighbour // 2, slot // 2)
        received.append(lax.ppermute(received[held[neighbour]], "dom", [hop]))
    count = len(received)
    early = finish(facts, [own] + received[:-1], noise, text, places, count)
    return tuple(finish(facts, received[-1:], noise, text, places, count, early))


def per_device(
    counts, video_query, video_key, video_value, text_query, text_key, text_value, fresh_noise
):
    resident, rows, features = video_query.shape
    text = text_query.shape[1]
    heads = features // HD
    known = plans(counts.shape[0])

    packed = pack(
        (video_query, video_key, video_value, text_query, text_key, text_value)
    )
    gathered = lax.all_to_all(packed, "seq", split_axis=0, concat_axis=0, tiled=True)
    attended = attend(gathered, rows, text)
    facts, plan = find_facts(counts, attended, [entry[0] for entry in known])
    returned = lax.all_to_all(attended, "seq", split_axis=0, concat_axis=0, tiled=True)
    own = returned.reshape(resident, heads, rows + text, HD)
    branches = [functools.partial(resample, *entry[1:], text) for entry in known]
    return lax.switch(plan[0], branches, facts, own, fresh_noise)


def solution(mesh):
    placed = P(("rep", "dom"), "seq", None)
    return jax.shard_map(
        per_device,
        mesh=mesh,
        in_specs=(P("rep"),) + (placed,) * 7,
        out_specs=(placed, placed),
        check_vma=False,
    )
```
